32 devices in a mesh: rep: 4 (over z), seq: 4 (over y, core), shard: 2 (over x).
Axes of the slice: x: 2, y: 2, z: 4, core: 2. Of those that a mesh axis runs over, the one named last changes fastest.
Arguments:
- tokens: bfloat16 [8, 1024, 1024], P(('rep', 'shard'), 'seq'), may hold values from -6 to 6
- cotangent: bfloat16 [8, 1024, 1024], P(('rep', 'shard'), 'seq'), may hold values from -6 to 6
- in_proj: bfloat16 [1024, 3072], P('shard'), may hold values from -0.1875 to 0.1875
- in_moment: bfloat16 [1024, 3072], P('shard'), may hold values from -64 to 64
- in_square: bfloat16 [1024, 3072], P('shard'), may hold values from 434 to 1720
- out_proj: bfloat16 [1024, 1024], P('shard'), may hold values from -0.1875 to 0.1875
- out_moment: bfloat16 [1024, 1024], P('shard'), may hold values from -80 to 80
- out_square: bfloat16 [1024, 1024], P('shard'), may hold values from 860 to 3440
- gate_up: bfloat16 [2, 1024, 4608], P(None, 'shard'), may hold values from -0.1875 to 0.1875
- gate_moment: bfloat16 [2, 1024, 4608], P(None, 'shard'), may hold values from -20 to 20
- gate_square: bfloat16 [2, 1024, 4608], P(None, 'shard'), may hold values from 43.25 to 172
- down_proj: bfloat16 [4608, 1024], P(None, 'shard'), may hold values from -0.09375 to 0.09375
- down_moment: bfloat16 [4608, 1024], P(None, 'shard'), may hold values from -40 to 40
- down_square: bfloat16 [4608, 1024], P(None, 'shard'), may hold values from 172 to 688
- conv_kernel: bfloat16 [3, 1024], P(None, 'shard'), may hold values from -3.5 to 3.5
- conv_moment: bfloat16 [3, 1024], P(None, 'shard'), may hold values from -80 to 80
- conv_square: bfloat16 [3, 1024], P(None, 'shard'), may hold values from 860 to 3440
- norm_gains: bfloat16 [2, 1024], P(None, 'shard'), may hold values from 0.5 to 1.5
- gains_moment: bfloat16 [2, 1024], P(None, 'shard'), may hold values from -80 to 80
- gains_square: bfloat16 [2, 1024], P(None, 'shard'), may hold values from 860 to 3440
Outputs:
- block_out: bfloat16 [8, 1024, 1024], P(('rep', 'shard'), 'seq')
- token_grad: bfloat16 [8, 1024, 1024], P(('rep', 'shard'), 'seq')
- in_next: float32 [1024, 3072], P('shard')
- in_moment_next: float32 [1024, 3072], P('shard')
- in_square_next: float32 [1024, 3072], P('shard')
- out_next: float32 [1024, 1024], P('shard')
- out_moment_next: float32 [1024, 1024], P('shard')
- out_square_next: float32 [1024, 1024], P('shard')
- gate_next: float32 [2, 1024, 4608], P(None, 'shard')
- gate_moment_next: float32 [2, 1024, 4608], P(None, 'shard')
- gate_square_next: float32 [2, 1024, 4608], P(None, 'shard')
- down_next: float32 [4608, 1024], P(None, 'shard')
- down_moment_next: float32 [4608, 1024], P(None, 'shard')
- down_square_next: float32 [4608, 1024], P(None, 'shard')
- conv_next: float32 [3, 1024], P(None, 'shard')
- conv_moment_next: float32 [3, 1024], P(None, 'shard')
- conv_square_next: float32 [3, 1024], P(None, 'shard')
- gains_next: float32 [2, 1024], P(None, 'shard')
- gains_moment_next: float32 [2, 1024], P(None, 'shard')
- gains_square_next: float32 [2, 1024], P(None, 'shard')
The draws below stay inside these ranges and needn't reach their ends.
All inputs are finite; a program needn't handle non-finite values.
Results may differ from the reference program's by a relative error of at most 0.008.
Values may be sent and summed in bfloat16 or wider, within the bound.
A program may use at most 512 MiB of HBM per device.

```python
import math
import jax
import jax.numpy as jnp
from jax import lax

D = 1024
FF = 4608
STEP = 10
SEQS = 8
LENGTH = 1024
TOKENS = 8192


def levels(rng, dims, split, smallest, high):
    loudness = 1.0
    for dim, shards_of in split:
        steps = jax.random.uniform(jax.random.fold_in(jax.random.fold_in(rng, 6), dim), (shards_of,), jnp.float32, smallest / len(split), high / len(split))
        loudness = loudness * jnp.repeat(jnp.exp(steps), dims[dim] // shards_of).reshape((-1,) + (1,) * (len(dims) - 1 - dim))
    return loudness


def noise(own_key, shape, scale, reach, split=(), kind=jnp.bfloat16):
    values = jax.random.normal(own_key, shape, jnp.float32) * scale
    if len(split) > 0:
        values = levels(own_key, shape, split, -0.22, 0.18) * values
    return jnp.clip(values, min=-reach, max=reach).astype(kind)


def setup_inputs(seed: int = 0) -> dict:
    key_list = jax.random.split(jax.random.key(seed), 21)
    tokens = noise(key_list[0], (SEQS, LENGTH, D), 1.0, 6.0, ((0, 8), (1, 4)))
    cotangent = noise(key_list[1], (SEQS, LENGTH, D), 1.0, 6.0, ((0, 8), (1, 4)))
    in_proj = noise(key_list[2], (D, 3 * D), D ** -0.5, 0.1875, ((0, 2),))
    in_moment = noise(key_list[3], (D, 3 * D), (0.111 * TOKENS ** 0.5), 64.0, ((0, 2),))
    in_square = jnp.clip(jnp.exp(math.log(1720.0) - 1.377035 * jax.random.uniform(key_list[4], (D, 3 * D), jnp.float32) ** levels(key_list[4], (D, 3 * D), ((0, 2),), -0.2, 0.2)), 434.0, 1720.0).astype(jnp.bfloat16)
    out_proj = noise(key_list[5], (D, D), D ** -0.5, 0.1875, ((0, 2),))
    out_moment = noise(key_list[6], (D, D), (0.157 * TOKENS ** 0.5), 80.0, ((0, 2),))
    out_square = jnp.clip(jnp.exp(math.log(3440.0) - 1.3862944 * jax.random.uniform(key_list[7], (D, D), jnp.float32) ** levels(key_list[7], (D, D), ((0, 2),), -0.2, 0.2)), 860.0, 3440.0).astype(jnp.bfloat16)
    gate_up = noise(key_list[8], (2, D, FF), D ** -0.5, 0.1875, ((1, 2),))
    gate_moment = noise(key_list[9], (2, D, FF), (0.035 * TOKENS ** 0.5), 20.0, ((1, 2),))
    gate_square = jnp.clip(jnp.exp(math.log(172.0) - 1.3804972 * jax.random.uniform(key_list[10], (2, D, FF), jnp.float32) ** levels(key_list[10], (2, D, FF), ((1, 2),), -0.2, 0.2)), 43.25, 172.0).astype(jnp.bfloat16)
    down_proj = noise(key_list[11], (FF, D), FF ** -0.5, 0.09375, ((1, 2),))
    down_moment = noise(key_list[12], (FF, D), (0.07 * TOKENS ** 0.5), 40.0, ((1, 2),))
    down_square = jnp.clip(jnp.exp(math.log(688.0) - 1.3862944 * jax.random.uniform(key_list[13], (FF, D), jnp.float32) ** levels(key_list[13], (FF, D), ((1, 2),), -0.2, 0.2)), 172.0, 688.0).astype(jnp.bfloat16)
    conv_kernel = noise(key_list[14], (3, D), 0.6, 3.5, ((1, 2),))
    conv_moment = noise(key_list[15], (3, D), (0.157 * TOKENS ** 0.5), 80.0, ((1, 2),))
    conv_square = jnp.clip(jnp.exp(math.log(3440.0) - 1.3862944 * jax.random.uniform(key_list[16], (3, D), jnp.float32) ** levels(key_list[16], (3, D), ((1, 2),), -0.2, 0.2)), 860.0, 3440.0).astype(jnp.bfloat16)
    norm_gains = jnp.clip(1.0 + 0.1 * jax.random.normal(key_list[17], (2, D), jnp.float32), 0.5, 1.5).astype(jnp.bfloat16)
    gains_moment = noise(key_list[18], (2, D), (0.157 * TOKENS ** 0.5), 80.0, ((1, 2),))
    gains_square = jnp.clip(jnp.exp(math.log(3440.0) - 1.3862944 * jax.random.uniform(key_list[19], (2, D), jnp.float32) ** levels(key_list[19], (2, D), ((1, 2),), -0.2, 0.2)), 860.0, 3440.0).astype(jnp.bfloat16)
    return {"tokens": tokens, "cotangent": cotangent, "in_proj": in_proj, "in_moment": in_moment, "in_square": in_square, "out_proj": out_proj, "out_moment": out_moment, "out_square": out_square, "gate_up": gate_up, "gate_moment": gate_moment, "gate_square": gate_square, "down_proj": down_proj, "down_moment": down_moment, "down_square": down_square, "conv_kernel": conv_kernel, "conv_moment": conv_moment, "conv_square": conv_square, "norm_gains": norm_gains, "gains_moment": gains_moment, "gains_square": gains_square}


norm_eps = 1e-05
beta_one = 0.9
beta_two = 0.95
adam_eps = 1e-08
decay_rate = 0.1
small_rate = 0.4

@jax.custom_vjp
def low(v):
    return lax.optimization_barrier(v.astype(jnp.bfloat16)).astype(jnp.float32)

@jax.custom_vjp
def low_back(v):
    return v

def low_keep(v):
    return (low(v), None)

def low_pass(kept, grad):
    return (grad,)

def back_keep(v):
    return (v, None)

def back_low(kept, grad):
    return (low(grad),)
low.defvjp(low_keep, low_pass)
low_back.defvjp(back_keep, back_low)

def matmul(left_side, right_side):
    return jnp.dot(left_side, right_side, precision=lax.Precision.HIGHEST)

def rms_norm(values, gain_vector):
    norm_scale = lax.rsqrt(lax.optimization_barrier(jnp.mean(values * values, axis=-1, keepdims=True)) + norm_eps)
    return values * norm_scale * gain_vector

def block(inputs, in_weight, out_weight, gate_weight, down_weight, conv_weight, gains_weight):
    normed_one = low(rms_norm(inputs, gains_weight[0]))
    projected = low_back(matmul(normed_one, in_weight))
    first_gate = projected[:, :D]
    second_gate = projected[:, D:2 * D]
    conv_input = projected[:, 2 * D:]
    mixed_in = low(first_gate * conv_input)
    padded = jnp.concatenate([jnp.zeros((2, D), mixed_in.dtype), mixed_in], axis=0)
    convolved = conv_weight[0] * padded[:-2] + conv_weight[1] * padded[1:-1] + conv_weight[2] * padded[2:]
    gated_out = low(second_gate * convolved)
    middle = inputs + low_back(matmul(gated_out, out_weight))
    normed_two = low(rms_norm(middle, gains_weight[1]))
    gate_value = low_back(matmul(normed_two, gate_weight[0]))
    upward = low_back(matmul(normed_two, gate_weight[1]))
    hidden = low(jax.nn.silu(gate_value) * upward)
    return middle + low_back(matmul(hidden, down_weight))

def adamw(weight, first_moment, second_moment, gradient, step_rate, decay_factor):
    first_new = beta_one * first_moment + (1.0 - beta_one) * gradient
    second_new = beta_two * second_moment + (1.0 - beta_two) * gradient * gradient
    adam_ratio = first_new / (1.0 - beta_one ** STEP) / (jnp.sqrt(second_new / (1.0 - beta_two ** STEP)) + adam_eps)
    weight_new = weight - step_rate * (adam_ratio + decay_factor * weight)
    return (weight_new, first_new, second_new)

def reference(tokens, cotangent, in_proj, in_moment, in_square, out_proj, out_moment, out_square, gate_up, gate_moment, gate_square, down_proj, down_moment, down_square, conv_kernel, conv_moment, conv_square, norm_gains, gains_moment, gains_square):
    weights = tuple((array.astype(jnp.float32) for array in (in_proj, out_proj, gate_up, down_proj, conv_kernel, norm_gains)))

    def one_sequence(carry, sequence):
        inputs, incoming = sequence
        result, pull = jax.vjp(block, inputs.astype(jnp.float32), *weights)
        grads = pull(incoming.astype(jnp.float32))
        carry = tuple((total + piece for total, piece in zip(carry, grads[1:])))
        return (carry, (result.astype(jnp.bfloat16), grads[0].astype(jnp.bfloat16)))
    zeros = tuple((jnp.zeros(array.shape, jnp.float32) for array in weights))
    totals, (block_out, token_grad) = lax.scan(one_sequence, zeros, (tokens, cotangent))
    matrix_rate = 2.0 * D ** (-0.5)
    down_rate = 2.0 * FF ** (-0.5)
    in_next, in_moment_next, in_square_next = adamw(weights[0], in_moment.astype(jnp.float32), in_square.astype(jnp.float32), totals[0], matrix_rate, decay_rate)
    out_next, out_moment_next, out_square_next = adamw(weights[1], out_moment.astype(jnp.float32), out_square.astype(jnp.float32), totals[1], matrix_rate, decay_rate)
    gate_next, gate_moment_next, gate_square_next = adamw(weights[2], gate_moment.astype(jnp.float32), gate_square.astype(jnp.float32), totals[2], matrix_rate, decay_rate)
    down_next, down_moment_next, down_square_next = adamw(weights[3], down_moment.astype(jnp.float32), down_square.astype(jnp.float32), totals[3], down_rate, decay_rate)
    conv_next, conv_moment_next, conv_square_next = adamw(weights[4], conv_moment.astype(jnp.float32), conv_square.astype(jnp.float32), totals[4], small_rate, 0.0)
    gains_next, gains_moment_next, gains_square_next = adamw(weights[5], gains_moment.astype(jnp.float32), gains_square.astype(jnp.float32), totals[5], small_rate, 0.0)
    return (block_out, token_grad, in_next, in_moment_next, in_square_next, out_next, out_moment_next, out_square_next, gate_next, gate_moment_next, gate_square_next, down_next, down_moment_next, down_square_next, conv_next, conv_moment_next, conv_square_next, gains_next, gains_moment_next, gains_square_next)
```

```python
import functools

import jax
import jax.numpy as jnp
from jax import lax
from jax.experimental import pallas as pl
from jax.experimental.pallas import tpu as pltpu
from jax.sharding import PartitionSpec as P

STEP = 10
norm_eps = 1e-05
beta_one = 0.9
beta_two = 0.95
adam_eps = 1e-08
decay_rate = 0.1
small_rate = 0.4

BF = jnp.bfloat16
F32 = jnp.float32
MESH = pl.DeviceIdType.MESH
CHUNK = 64
LAGS = (0, 2, 4, 6, 9)
PARTS = {"in": 1, "out": 1, "gate": 2, "up": 2, "down": 4}
TILE = 16

NAMES = (
    "small", "in_0", "out_0", "gate_0", "gate_1", "up_0", "up_1", "down_0", "down_1", "down_2", "down_3",
    "in_0_z", "out_0_z", "gate_0_z", "gate_1_z", "up_0_z", "up_1_z", "down_0_z", "down_1_z", "down_2_z",
    "down_3_z", "n1_c", "n1_y", "n1_f", "n2_c", "n2_y", "n2_f", "ct_c", "ct_y", "ct_f", "ml_c", "ml_y",
    "ml_f", "ro_0", "ro_1", "ro_y", "rg_0", "rg_1", "rg_y", "rr_0", "rr_1", "rr_y", "ri_0", "ri_1", "ri_y",
    "sg_x", "sg_c", "sg_y", "sg_a", "sg_b", "sg_t",
)
LOCALS = (
    "tok", "small", "ct", "in", "out", "gate", "up", "down",
)


def dot(a, b):
    return lax.dot_general(a, b, (((1,), (0,)), ((), ())), preferred_element_type=F32)


def dot_nt(a, b):
    return lax.dot_general(a, b, (((1,), (1,)), ((), ())), preferred_element_type=F32)


def dot_tn(a, b):
    return lax.dot_general(a, b, (((0,), (0,)), ((), ())), preferred_element_type=F32)


def block_kernel(
    dims,
    tok_h, cot_h, in_h, out_h, gu_h, dn_h, small_h,
    block_out, token_grad, grads, small_grads,
    WG, WD, WIN, WOUT, SM, TOK, N1, N2, CT, ML,
    PROJ, MX, CONV, GATED, GCO, ACT, FA, GS, GO, RX,
    MID, GM, P32, SC, RC, SY, RY, SG,
    ss, rs, ls, xs, xr, z1s, z1r, z2s, z2r, ts, tr, ys, yr, c1s, c1r, c2s, c2r, gl,
    ready_w, ready_a,
):
    D, T, FQ, F = dims
    H, Q, R = D // 2, FQ // 2, 4 * T
    MT = H // 2
    NCH = 2 * D // CHUNK
    z = lax.axis_index("rep")
    s = lax.axis_index("seq")
    x = lax.axis_index("shard")
    y, c = s // 2, s % 2
    h = z % 2
    is_mid = jnp.logical_and(z > 0, z < 3)
    is_end = jnp.logical_or(z == 0, z == 3)
    xo = 1 - x
    xp = (z, s, xo)
    cp = (z, 2 * y + 1 - c, x)
    yp = (z, 2 * (1 - y) + c, x)
    zp = (z + 1 - 2 * h, s, x)
    mp = (3 - z, s, x)

    def block(i):
        return 2 * (y + (i // 2) * (1 - 2 * y)) + c + (i % 2) * (1 - 2 * c)

    def rows(m, n=T):
        return pl.ds(pl.multiple_of(m * n, n), n)

    def at(start, size, unit):
        return pl.ds(pl.multiple_of(start, unit), size)

    def remote(name, src, dst, dev):
        k = NAMES.index(name)
        return pltpu.make_async_remote_copy(
            src_ref=src, dst_ref=dst, send_sem=ss.at[k], recv_sem=rs.at[k], device_id=dev, device_id_type=MESH
        )

    def local(name, src, dst):
        return pltpu.make_async_copy(src, dst, ls.at[LOCALS.index(name)])

    barrier = pltpu.get_barrier_semaphore()
    for dev in (xp, cp, yp, zp):
        pl.semaphore_signal(barrier, inc=1, device_id=dev, device_id_type=MESH)

    @pl.when(is_mid)
    def _():
        pl.semaphore_signal(barrier, inc=1, device_id=mp, device_id_type=MESH)

    loads = [
        local("tok", tok_h, TOK),
        local("small", small_h, SM.at[x]),
        local("ct", cot_h, CT.at[rows(s)]),
    ]
    for j in range(3):
        for k in range(2):
            loads.append(
                local(
                    "in",
                    in_h.at[:, at(D * j + H * k + Q * s, Q, Q)],
                    WIN.at[rows(x, H), pl.ds(FQ * j + Q * k, Q)],
                )
            )
    loads.append(local("out", out_h.at[rows(s, Q)], WOUT.at[rows(x, Q)]))
    for j, name in enumerate(("gate", "up")):
        loads.append(
            local(name, gu_h.at[j, :, at(F * s, F, 128)], WG.at[at(D * j + H * x, H, H)])
        )
    loads.append(local("down", dn_h.at[rows(s, F)], WD.at[:, at(H * x, H, H)]))
    for copy in loads:
        copy.start()

    def local_wait(name):
        whole = {
            "tok": lambda: local("tok", tok_h, TOK),
            "small": lambda: local("small", small_h, SM.at[x]),
            "ct": lambda: local("ct", cot_h, CT.at[rows(s)]),
            "in": lambda: local("in", WIN.at[rows(x, H)], WIN.at[rows(x, H)]),
            "out": lambda: local("out", WOUT.at[rows(x, Q)], WOUT.at[rows(x, Q)]),
            "gate": lambda: local("gate", WG.at[at(H * x, H, H)], WG.at[at(H * x, H, H)]),
            "up": lambda: local("up", WG.at[at(D + H * x, H, H)], WG.at[at(D + H * x, H, H)]),
            "down": lambda: local("down", WD.at[:, at(H * x, H, H)], WD.at[:, at(H * x, H, H)]),
        }
        whole[name]().wait()

    @pl.when(is_mid)
    def _():
        pl.semaphore_wait(barrier, 5)

    @pl.when(is_end)
    def _():
        pl.semaphore_wait(barrier, 4)

    def part(name, owner, half, p):
        if name == "in":
            return WIN.at[at(H * owner + (H // 2) * half, H // 2, H // 2)]
        if name == "out":
            return WOUT.at[at(Q * owner + (Q // 2) * half, Q // 2, Q // 2)]
        if name == "down":
            n = F // 2 // PARTS[name]
            return WD.at[at((F // 2) * half + n * p, n, 16), at(H * owner, H, H)]
        j = 0 if name == "gate" else 1
        n = H // 2 // PARTS[name]
        return WG.at[at(D * j + H * owner + (H // 2) * half + n * p, n, n)]

    def weight_send(name):
        if name == "in":
            for j in range(3):
                for k in range(2):
                    remote(
                        "in_0",
                        in_h.at[at((H // 2) * h, H // 2, H // 2), at(D * j + H * k + Q * s, Q, Q)],
                        WIN.at[at(H * x + (H // 2) * h, H // 2, H // 2), pl.ds(FQ * j + Q * k, Q)],
                        xp,
                    ).start()
            return
        for p in range(PARTS[name]):
            if name == "out":
                src = out_h.at[at(Q * s + (Q // 2) * h, Q // 2, Q // 2)]
            elif name == "down":
                n = F // 2 // PARTS[name]
                src = dn_h.at[at(F * s + (F // 2) * h + n * p, n, 16)]
            else:
                n = H // 2 // PARTS[name]
                src = gu_h.at[0 if name == "gate" else 1, at((H // 2) * h + n * p, n, n), at(F * s, F, 128)]
            remote(name + "_" + str(p), src, part(name, x, h, p), xp).start()

    def weight_pass(name):
        for p in range(PARTS[name]):
            here = part(name, xo, h, p)
            remote(name + "_" + str(p), here, here, xp).wait_recv()
            remote(name + "_" + str(p) + "_z", here, here, zp).start()

    def weight_wait(name):
        local_wait(name)
        for p in range(PARTS[name]):
            there = part(name, xo, 1 - h, p)
            remote(name + "_" + str(p) + "_z", there, there, zp).wait_recv()

    def weight_sent(name):
        for p in range(PARTS[name]):
            here = part(name, x, h, p)
            remote(name + "_" + str(p), here, here, xp).wait_send()

    def weight_passed(name):
        for p in range(PARTS[name]):
            here = part(name, xo, h, p)
            remote(name + "_" + str(p) + "_z", here, here, zp).wait_send()

    remote("small", small_h, SM.at[x], xp).start()
    weight_send("in")
    weight_send("out")
    weight_send("gate")
    weight_send("up")
    weight_send("down")

    def gather_copy(name, buf, kind):
        m = block(2) if kind == "f" else s
        return remote(name + "_" + kind, buf.at[rows(m)], buf.at[rows(m)], yp if kind == "y" else cp)

    def gather_start(name, buf):
        gather_copy(name, buf, "y").start()
        gather_copy(name, buf, "c").start()

    def gather_step(name, buf, i):
        @pl.when(i == 1)
        def _():
            remote(name + "_c", buf.at[rows(block(1))], buf.at[rows(block(1))], cp).wait_recv()

        @pl.when(i == 2)
        def _():
            remote(name + "_y", buf.at[rows(block(2))], buf.at[rows(block(2))], yp).wait_recv()
            gather_copy(name, buf, "f").start()

        @pl.when(i == 3)
        def _():
            remote(name + "_f", buf.at[rows(block(3))], buf.at[rows(block(3))], cp).wait_recv()

    def sum_core(name, lot, k):
        return remote(name + "_" + str(k), SC.at[lot, k], RC.at[lot, k], cp)

    def sum_y(name, lot):
        return remote(name + "_y", SY.at[lot], RY.at[lot], yp)

    def sum_emit(name, lot, i, partial):
        @pl.when(i % 2 == 0)
        def _():
            P32[i // 2] = partial

        @pl.when(i == 1)
        def _():
            SC[lot, 1] = partial.astype(BF)
            sum_core(name, lot, 1).start()

        @pl.when(i == 3)
        def _():
            SC[lot, 0] = partial.astype(BF)
            sum_core(name, lot, 0).start()

    def sum_cross(name, lot):
        sum_core(name, lot, 0).wait_recv()
        SY[lot] = (P32[1] + RC[lot, 0].astype(F32)).astype(BF)
        sum_y(name, lot).start()

    def sum_wait(name, lot):
        sum_core(name, lot, 1).wait_recv()
        sum_y(name, lot).wait_recv()

    def sum_rows(lot, r):
        return P32[0, r] + RC[lot, 1, r].astype(F32) + RY[lot, r].astype(F32)

    def sum_done(name, lot):
        sum_core(name, lot, 0).wait_send()
        sum_core(name, lot, 1).wait_send()
        sum_y(name, lot).wait_send()

    def tiles(n, body, size=TILE):
        def step(t, carry):
            body(pl.ds(pl.multiple_of(t * size, size), size))
            return carry

        lax.fori_loop(0, n // size, step, 0)

    def blocks(body, first=0, last=4):
        def step(i, carry):
            body(i, block(i))
            return carry

        lax.fori_loop(first, last, step, 0)

    def gain(k):
        return jnp.concatenate([SM[0, 3 + k : 4 + k, :], SM[1, 3 + k : 4 + k, :]], axis=1)

    def tap(k):
        cols = rows(s, Q)
        return jnp.concatenate([SM[0, k : k + 1, cols], SM[1, k : k + 1, cols]], axis=1)

    local_wait("tok")
    local_wait("small")
    remote("small", small_h, SM.at[xo], xp).wait()
    SG[0] = jnp.zeros_like(SG[0])

    gain_one = gain(0)

    def norm_one(r):
        v = TOK[r].astype(F32)
        scale = lax.rsqrt(jnp.mean(v * v, axis=-1, keepdims=True) + norm_eps)
        N1[pl.ds(pl.multiple_of(s * T + r.start, TILE), TILE)] = (v * scale * gain_one).astype(BF)

    tiles(T, norm_one)
    gather_start("n1", N1)
    local_wait("ct")
    gather_start("ct", CT)

    MX[0:8] = jnp.zeros((8, FQ), F32)
    GCO[R : R + 8] = jnp.zeros((8, FQ), F32)
    weight_pass("in")
    weight_pass("out")
    weight_wait("in")

    def project(i, m):
        gather_step("n1", N1, i)
        p = dot(N1[rows(m)], WIN[...])
        PROJ[rows(m)] = p
        mixed = (p[:, :FQ] * p[:, 2 * FQ :]).astype(BF)
        MX[at(8 + m * T, T, 8)] = mixed.astype(F32)

    blocks(project)
    weight_wait("out")

    def convolve(i, m):
        i = 3 - i
        m = block(i)
        ext = MX[at(m * T, T + 8, 8)]
        conv = tap(0) * ext[6 : 6 + T] + tap(1) * ext[7 : 7 + T] + tap(2) * ext[8 : 8 + T]
        CONV[rows(m)] = conv
        gated = (PROJ[rows(m), FQ : 2 * FQ] * conv).astype(BF)
        GATED[rows(m)] = gated
        sum_emit("ro", 0, i, dot(gated, WOUT[...]))

    blocks(convolve)
    sum_cross("ro", 0)
    weight_pass("gate")
    sum_wait("ro", 0)

    gain_two = gain(1)

    def norm_two(r):
        v = TOK[r].astype(F32) + sum_rows(0, r)
        MID[r] = v
        scale = lax.rsqrt(jnp.mean(v * v, axis=-1, keepdims=True) + norm_eps)
        N2[pl.ds(pl.multiple_of(s * T + r.start, TILE), TILE)] = (v * scale * gain_two).astype(BF)

    tiles(T, norm_two)
    gather_start("n2", N2)
    sum_done("ro", 0)
    weight_pass("up")
    weight_pass("down")
    weight_wait("gate")
    weight_wait("up")
    weight_wait("down")

    def feed(i, m):
        gather_step("n2", N2, i)
        gather_step("ct", CT, i)
        FA[0] = dot(N2[rows(m)], WG[0:D])
        FA[1] = dot(N2[rows(m)], WG[D : 2 * D])
        FA[2] = dot_nt(CT[rows(m)], WD[...])

        def act(r):
            gate, up, gh = FA[0, r], FA[1, r], FA[2, r]
            sig = jax.nn.sigmoid(gate)
            silu = gate * sig
            ro = pl.ds(pl.multiple_of(m * T + r.start, TILE), TILE)
            ACT[ro] = (gh * up * sig * (1.0 + gate * (1.0 - sig))).astype(BF)
            ro = pl.ds(pl.multiple_of(R + m * T + r.start, TILE), TILE)
            ACT[ro] = (gh * silu).astype(BF)
            ro = pl.ds(pl.multiple_of(2 * R + m * T + r.start, TILE), TILE)
            ACT[ro] = (silu * up).astype(BF)

        tiles(T, act)
        partial = dot_nt(ACT[rows(m)], WG[0:D]) + dot_nt(ACT[at(R + m * T, T, T)], WG[D : 2 * D])
        sum_emit("rg", 1, i, partial)

    blocks(feed)
    sum_cross("rg", 1)
    weight_passed("gate")
    weight_passed("up")
    pl.semaphore_signal(ready_w, inc=1, device_id=zp, device_id_type=MESH)

    def chunk(k):
        return rows(k, CHUNK)

    def x_copy(k):
        return pltpu.make_async_remote_copy(
            src_ref=GS.at[chunk(k)], dst_ref=RX.at[chunk(k)], send_sem=xs.at[k], recv_sem=xr.at[k],
            device_id=xp, device_id_type=MESH,
        )

    def z1_copy(k):
        return pltpu.make_async_remote_copy(
            src_ref=GO.at[chunk(k)], dst_ref=WG.at[chunk(k)], send_sem=z1s.at[k], recv_sem=z1r.at[k],
            device_id=zp, device_id_type=MESH,
        )

    def z2_copy(k):
        return pltpu.make_async_remote_copy(
            src_ref=RX.at[chunk(k)], dst_ref=ACT.at[chunk(k)], send_sem=z2s.at[k], recv_sem=z2r.at[k],
            device_id=mp, device_id_type=MESH,
        )

    def t_copy(k):
        return pltpu.make_async_remote_copy(
            src_ref=GO.at[chunk(k)], dst_ref=WG.at[chunk(k)], send_sem=ts.at[k], recv_sem=tr.at[k],
            device_id=zp, device_id_type=MESH,
        )

    def y_copy(k, src):
        return pltpu.make_async_remote_copy(
            src_ref=src.at[chunk(k)], dst_ref=grads.at[s, chunk(k)], send_sem=ys.at[k], recv_sem=yr.at[k],
            device_id=yp, device_id_type=MESH,
        )

    def c1_copy(k, src):
        return pltpu.make_async_remote_copy(
            src_ref=src.at[chunk(k)], dst_ref=grads.at[s, chunk(k)], send_sem=c1s.at[k], recv_sem=c1r.at[k],
            device_id=cp, device_id_type=MESH,
        )

    def c2_copy(k):
        m = block(2)
        return pltpu.make_async_remote_copy(
            src_ref=grads.at[m, chunk(k)], dst_ref=grads.at[m, chunk(k)], send_sem=c2s.at[k], recv_sem=c2r.at[k],
            device_id=cp, device_id_type=MESH,
        )

    def own_copy(k, src):
        return pltpu.make_async_copy(src.at[chunk(k)], grads.at[s, chunk(k)], gl.at[k])

    def add_rows(k, dst, one, two):
        def step(t, carry):
            r = pl.ds(pl.multiple_of(k * CHUNK + t * TILE, TILE), TILE)
            dst[r] = (one[r].astype(F32) + two[r].astype(F32)).astype(BF)
            return carry

        lax.fori_loop(0, CHUNK // TILE, step, 0)

    def tick(k):
        def stage(lag, body):
            pl.when(jnp.logical_and(k >= lag, k < NCH + lag))(lambda: body(k - lag))

        def add_x(k):
            x_copy(k).wait_recv()
            add_rows(k, GO, GO, RX)
            pl.when(is_end)(lambda: z1_copy(k).start())

        def add_end(k):
            @pl.when(is_mid)
            def _():
                z1_copy(k).wait_recv()
                add_rows(k, RX, GO, WG)
                z2_copy(k).start()

        def spread(k, src):
            y_copy(k, src).start()
            c1_copy(k, src).start()
            own_copy(k, src).start()

        def add_mid(k):
            @pl.when(is_mid)
            def _():
                z2_copy(k).wait_recv()
                add_rows(k, GO, RX, ACT)
                t_copy(k).start()
                spread(k, GO)

        def take(k):
            @pl.when(is_end)
            def _():
                t_copy(k).wait_recv()
                spread(k, WG)

        def hand(k):
            m = block(2)
            pltpu.make_async_remote_copy(
                src_ref=grads.at[m, chunk(k)], dst_ref=grads.at[m, chunk(k)], send_sem=ys.at[k], recv_sem=yr.at[k],
                device_id=yp, device_id_type=MESH,
            ).wait_recv()
            c2_copy(k).start()

        for body, lag in zip((add_x, add_end, add_mid, take, hand), LAGS):
            stage(lag, body)

    def ticks(first, last):
        def step(k, carry):
            tick(k)
            return carry

        lax.fori_loop(first, last, step, 0)

    def weight_grad(row, left, right, cols, dst, owner):
        def step(t, carry):
            lhs = left[:, at(H * owner + MT * t, MT, MT)]
            dst[at(row + MT * t, MT, MT), 0:cols] = dot_tn(lhs, right()).astype(BF)
            return carry

        lax.fori_loop(0, H // MT, step, 0)

    def act_at(j):
        return lambda: ACT[j * R : (j + 1) * R]

    def send(first, last):
        for k in range(first, last):
            x_copy(k).start()

    n_arr = H // CHUNK
    weight_grad(0, N2, act_at(0), F, GS, xo)
    send(0, n_arr)
    weight_grad(H, N2, act_at(1), F, GS, xo)
    send(n_arr, 2 * n_arr)
    weight_grad(2 * H, CT, act_at(2), F, GS, xo)
    send(2 * n_arr, 3 * n_arr)
    weight_grad(0, N2, act_at(0), F, GO, x)
    weight_grad(H, N2, act_at(1), F, GO, x)
    weight_grad(2 * H, CT, act_at(2), F, GO, x)

    @pl.when(is_mid)
    def _():
        pl.semaphore_signal(ready_a, inc=1, device_id=mp, device_id_type=MESH)

    pl.semaphore_wait(ready_w, 1)

    @pl.when(is_mid)
    def _():
        pl.semaphore_wait(ready_a, 1)

    ticks(0, 3)

    sum_wait("rg", 1)

    def back_two(t, acc):
        r = pl.ds(pl.multiple_of(t * TILE, TILE), TILE)
        v = MID[r]
        scale = lax.rsqrt(jnp.mean(v * v, axis=-1, keepdims=True) + norm_eps)
        unit = v * scale
        e = sum_rows(1, r)
        eu = e * unit
        ew = e * gain_two
        grad = scale * (ew - unit * jnp.mean(ew * unit, axis=-1, keepdims=True))
        ro = pl.ds(pl.multiple_of(s * T + t * TILE, TILE), TILE)
        gm = CT[ro].astype(F32) + grad
        GM[r] = gm
        ML[ro] = gm.astype(BF)
        return acc + jnp.sum(eu, axis=0, keepdims=True)

    SG[0, 4:5, :] = lax.fori_loop(0, T // TILE, back_two, jnp.zeros((1, D), F32))
    gather_start("ml", ML)
    sum_done("rg", 1)
    ticks(3, 7)

    def gated_back(i, m):
        gather_step("ml", ML, i)
        gg = dot_nt(ML[rows(m)], WOUT[...])
        gco = gg * PROJ[rows(m), FQ : 2 * FQ]
        GCO[rows(m)] = gco
        PROJ[rows(m), FQ : 2 * FQ] = gg * CONV[rows(m)]

    blocks(gated_back)
    for kind in "cyf":
        gather_copy("n2", N2, kind).wait_send()

    def conv_back(i, acc):
        m = block(i)
        gco = GCO[at(m * T, T + 8, 8)]
        ext = MX[at(m * T, T + 8, 8)]
        here = gco[0:T]
        gm = tap(2) * here + tap(1) * gco[1 : 1 + T] + tap(0) * gco[2 : 2 + T]
        p = PROJ[rows(m)]
        low = jnp.concatenate([gm * p[:, 2 * FQ :], p[:, FQ : 2 * FQ], gm * p[:, :FQ]], axis=1).astype(BF)
        N2[rows(m), 0 : 3 * FQ] = low
        sum_emit("ri", 1, i, dot_nt(low, WIN[...]))
        return tuple(
            a + jnp.sum(here * ext[6 + k : 6 + k + T], axis=0, keepdims=True) for k, a in enumerate(acc)
        )

    def conv_step(i, acc):
        return conv_back(3 - i, acc)

    conv_grads = lax.fori_loop(0, 4, conv_step, (jnp.zeros((1, FQ), F32),) * 3)
    for k in range(3):
        SG[0, k : k + 1, rows(s, Q)] = conv_grads[k][:, :Q]
        SG[0, k : k + 1, at(H + s * Q, Q, Q)] = conv_grads[k][:, Q:]
    sum_cross("ri", 1)

    def io_grad(dst, owner):
        def step(t, carry):
            lhs = N1[:, at(H * owner + MT * t, MT, MT)]
            dst[at(3 * H + MT * t, MT, MT), 0 : 3 * FQ] = dot_tn(lhs, N2[:, 0 : 3 * FQ]).astype(BF)
            right = GATED[:, rows(owner, Q)]
            for j in range(2):
                lhs = ML[:, at(H * j + MT * t, MT, MT)]
                dst[at(3 * H + MT * t, MT, MT), 3 * FQ + Q * j : 3 * FQ + Q * (j + 1)] = dot_tn(lhs, right).astype(BF)
            if 3 * FQ + 2 * Q < F:
                dst[at(3 * H + MT * t, MT, MT), 3 * FQ + 2 * Q : F] = jnp.zeros((MT, F - 3 * FQ - 2 * Q), BF)
            return carry

        lax.fori_loop(0, H // MT, step, 0)

    io_grad(GS, xo)
    send(3 * n_arr, NCH)
    ticks(7, 9)
    io_grad(GO, x)
    ticks(9, 11)

    sum_wait("ri", 1)
    TOKOUT = SC.at[0, 0]

    def back_one(t, acc):
        r = pl.ds(pl.multiple_of(t * TILE, TILE), TILE)
        v = TOK[r].astype(F32)
        scale = lax.rsqrt(jnp.mean(v * v, axis=-1, keepdims=True) + norm_eps)
        unit = v * scale
        e = sum_rows(1, r)
        eu = e * unit
        ew = e * gain_one
        grad = scale * (ew - unit * jnp.mean(ew * unit, axis=-1, keepdims=True))
        TOKOUT[r] = (GM[r] + grad).astype(BF)
        return acc + jnp.sum(eu, axis=0, keepdims=True)

    SG[0, 3:4, :] = lax.fori_loop(0, T // TILE, back_one, jnp.zeros((1, D), F32))
    out_copy = pltpu.make_async_copy(TOKOUT, token_grad, ls.at[LOCALS.index("tok")])
    out_copy.start()
    sum_done("ri", 1)
    ticks(11, 13)

    out_copy.wait()

    def down(i, m):
        i = 3 - i
        m = block(i)
        sum_emit("rr", 0, i, dot(ACT[at(2 * R + m * T, T, T)], WD[...]))

    blocks(down)
    sum_cross("rr", 0)

    def small_start(name, dev, k):
        remote(name, SG.at[0], SG.at[k], dev).start()

    def small_end(name, dev, k):
        remote(name, SG.at[0], SG.at[k], dev).wait()
        SG[0] = SG[0] + SG[k]

    small_start("sg_x", xp, 1)
    ticks(13, 15)
    small_end("sg_x", xp, 1)
    small_start("sg_c", cp, 2)
    ticks(15, 16)
    small_end("sg_c", cp, 2)
    small_start("sg_y", yp, 3)
    ticks(16, 19)
    small_end("sg_y", yp, 3)
    pl.when(is_end)(lambda: small_start("sg_a", zp, 4))
    ticks(19, 20)

    sum_wait("rr", 0)
    sum_done("rr", 0)

    def result(r):
        TOKOUT[r] = (MID[r] + sum_rows(0, r)).astype(BF)

    tiles(T, result)
    out_copy = pltpu.make_async_copy(TOKOUT, block_out, ls.at[LOCALS.index("tok")])
    out_copy.start()
    ticks(20, 22)

    @pl.when(is_mid)
    def _():
        remote("sg_a", SG.at[0], SG.at[4], zp).wait_recv()
        SG[0] = SG[0] + SG[4]
        small_start("sg_b", mp, 5)

    ticks(22, 25)

    @pl.when(is_end)
    def _():
        remote("sg_a", SG.at[0], SG.at[4], zp).wait_send()

    @pl.when(is_mid)
    def _():
        remote("sg_b", SG.at[0], SG.at[5], mp).wait()
        SG[6] = SG[0] + SG[5]
        remote("sg_t", SG.at[6], SG.at[6], zp).start()

    ticks(25, 30)

    @pl.when(is_mid)
    def _():
        remote("sg_t", SG.at[6], SG.at[6], zp).wait_send()

    @pl.when(is_end)
    def _():
        remote("sg_t", SG.at[6], SG.at[6], zp).wait_recv()

    small_copy = pltpu.make_async_copy(SG.at[6], small_grads, ls.at[LOCALS.index("small")])
    small_copy.start()
    ticks(30, NCH + LAGS[-1])

    def finish(k, carry):
        x_copy(k).wait_send()

        @pl.when(is_end)
        def _():
            z1_copy(k).wait_send()

        @pl.when(is_mid)
        def _():
            z2_copy(k).wait_send()
            t_copy(k).wait_send()

        y_copy(k, GO).wait_send()
        c1_copy(k, GO).wait()
        c2_copy(k).wait()
        own_copy(k, GO).wait()
        return carry

    lax.fori_loop(0, NCH, finish, 0)
    out_copy.wait()
    small_copy.wait()
    for name in ("in", "out", "gate", "up", "down"):
        weight_sent(name)
        if name not in ("gate", "up"):
            weight_passed(name)
    for name, buf in (("n1", N1), ("ct", CT), ("ml", ML)):
        for kind in "cyf":
            gather_copy(name, buf, kind).wait_send()


def run_block(tokens, cotangent, in_proj, out_proj, gate_up, down_proj, small):
    T, D = tokens.shape
    F = gate_up.shape[2] // 4
    FQ = D // 4
    R = 4 * T
    dims = (D, T, FQ, F)
    NCH = 2 * D // CHUNK
    hbm = pl.BlockSpec(memory_space=pltpu.HBM)
    dma = pltpu.SemaphoreType.DMA
    vmem = pltpu.VMEM
    scratch = [
        vmem((2 * D, F), BF),
        vmem((F, D), BF),
        vmem((D, 3 * FQ), BF),
        vmem((FQ, D), BF),
        vmem((2, 8, D // 2), F32),
        vmem((T, D), BF),
        vmem((R, D), BF),
        vmem((R, D), BF),
        vmem((R, D), BF),
        vmem((R, D), BF),
        vmem((R, 3 * FQ), F32),
        vmem((R + 8, FQ), F32),
        vmem((R, FQ), F32),
        vmem((R, FQ), BF),
        vmem((R + 8, FQ), F32),
        vmem((3 * R, F), BF),
        vmem((3, T, F), F32),
        vmem((2 * D, F), BF),
        vmem((2 * D, F), BF),
        vmem((2 * D, F), BF),
        vmem((T, D), F32),
        vmem((T, D), F32),
        vmem((2, T, D), F32),
        vmem((2, 2, T, D), BF),
        vmem((2, 2, T, D), BF),
        vmem((2, T, D), BF),
        vmem((2, T, D), BF),
        vmem((7, 8, D), F32),
        dma((len(NAMES),)),
        dma((len(NAMES),)),
        dma((len(LOCALS),)),
    ]
    scratch += [dma((NCH,))] * 15
    scratch += [pltpu.SemaphoreType.REGULAR, pltpu.SemaphoreType.REGULAR]
    flops = 6 * R * D * (3 * F + 4 * FQ) * 2
    return pl.pallas_call(
        functools.partial(block_kernel, dims),
        out_shape=(
            jax.ShapeDtypeStruct((T, D), BF),
            jax.ShapeDtypeStruct((T, D), BF),
            jax.ShapeDtypeStruct((4, 2 * D, F), BF),
            jax.ShapeDtypeStruct((8, D), F32),
        ),
        in_specs=[hbm] * 7,
        out_specs=(hbm,) * 4,
        scratch_shapes=scratch,
        compiler_params=pltpu.CompilerParams(
            collective_id=0, has_side_effects=True, vmem_limit_bytes=62 * 2**20
        ),
        cost_estimate=pl.CostEstimate(flops=flops, bytes_accessed=60 * 2**20, transcendentals=R * F),
        name="block_kernel",
    )(tokens, cotangent, in_proj, out_proj, gate_up, down_proj, small)


def adamw(weight, first_moment, second_moment, gradient, step_rate, decay_factor):
    first_new = beta_one * first_moment + (1.0 - beta_one) * gradient
    second_new = beta_two * second_moment + (1.0 - beta_two) * gradient * gradient
    adam_ratio = (
        first_new
        / (1.0 - beta_one**STEP)
        / (jnp.sqrt(second_new / (1.0 - beta_two**STEP)) + adam_eps)
    )
    weight_new = weight - step_rate * (adam_ratio + decay_factor * weight)
    return (weight_new, first_new, second_new)


def update_values(rate, w, m, v, grad):
    return adamw(w.astype(F32), m.astype(F32), v.astype(F32), grad.astype(F32), rate, decay_rate)


def update_plain(rate, w, m, v, g, *new):
    shape = w.shape
    flat = shape[-2:]
    values = update_values(rate, w[...].reshape(flat), m[...].reshape(flat), v[...].reshape(flat), g[...].reshape(flat))
    for ref, value in zip(new, values):
        ref[...] = value.reshape(shape)


def update_turned(rate, w, m, v, g, *new):
    values = update_values(rate, w[...], m[...], v[...], g[0].astype(F32).T)
    for ref, value in zip(new, values):
        ref[...] = value


def update_inner(rate, w, m, v, g, *new):
    n = g.shape[0]
    Q = w.shape[1] // (6 * n)
    for j in range(6):
        for k in range(n):
            cols = slice((n * j + k) * Q, (n * j + k + 1) * Q)
            values = update_values(rate, w[:, cols], m[:, cols], v[:, cols], g[k, :, Q * j : Q * (j + 1)])
            for ref, value in zip(new, values):
                ref[:, cols] = value


def update_outer(rate, w, m, v, g, *new):
    H, Q = g.shape[1], g.shape[2] // 2
    for j in range(2):
        cols = slice(H * j, H * (j + 1))
        grad = g[0, :, Q * j : Q * (j + 1)].astype(F32).T
        values = update_values(rate, w[:, cols], m[:, cols], v[:, cols], grad)
        for ref, value in zip(new, values):
            ref[:, cols] = value


def update(kernel, weight, first, second, grads, rate, grid, block, at, g_block, g_at, name):
    spec = pl.BlockSpec(block, at)
    n = weight.size
    return pl.pallas_call(
        functools.partial(kernel, rate),
        grid=grid,
        in_specs=[spec, spec, spec, pl.BlockSpec(g_block, g_at)],
        out_specs=(spec,) * 3,
        out_shape=(jax.ShapeDtypeStruct(weight.shape, F32),) * 3,
        compiler_params=pltpu.CompilerParams(vmem_limit_bytes=56 * 2**20),
        cost_estimate=pl.CostEstimate(flops=12 * n, bytes_accessed=20 * n, transcendentals=2 * n),
        name=name,
    )(weight, first, second, grads)


def fused_body(
    tokens, cotangent, in_proj, in_moment, in_square, out_proj, out_moment, out_square,
    gate_up, gate_moment, gate_square, down_proj, down_moment, down_square,
    conv_kernel, conv_moment, conv_square, norm_gains, gains_moment, gains_square,
):
    T, D = tokens.shape[1:]
    H, Q = D // 2, D // 8
    F = gate_up.shape[2] // 4
    FF = 4 * F
    rate = 2.0 * D ** (-0.5)
    down_rate = 2.0 * FF ** (-0.5)
    small = jnp.concatenate(
        [conv_kernel.astype(F32), norm_gains.astype(F32), jnp.zeros((3, H), F32)], axis=0
    )
    block_out, token_grad, grads, small_grads = run_block(
        tokens[0], cotangent[0], in_proj, out_proj, gate_up, down_proj, small
    )
    n = H // 256
    gate = update(
        update_plain, gate_up, gate_moment, gate_square, grads, rate,
        (2, n, 4), (1, 256, F), lambda j, r, k: (j, r, k),
        (1, 256, F), lambda j, r, k: (k, j * n + r, 0), "update_gate",
    )
    down = update(
        update_turned, down_proj, down_moment, down_square, grads, down_rate,
        (4, n), (F, 256), lambda k, r: (k, r),
        (1, 256, F), lambda k, r: (k, 2 * n + r, 0), "update_down",
    )
    inner = update(
        update_inner, in_proj, in_moment, in_square, grads, rate,
        (H // 64,), (64, 3 * D), lambda r: (r, 0),
        (4, 64, F), lambda r: (0, 3 * H // 64 + r, 0), "update_in",
    )
    outer = update(
        update_outer, out_proj, out_moment, out_square, grads, rate,
        (4,), (Q, D), lambda k: (k, 0),
        (1, H, 2 * Q), lambda k: (k, 3, 3), "update_out",
    )
    mine = lax.dynamic_slice_in_dim(small_grads, lax.axis_index("shard") * H, H, axis=1)
    conv = adamw(
        conv_kernel.astype(F32), conv_moment.astype(F32), conv_square.astype(F32), mine[0:3], small_rate, 0.0
    )
    gains = adamw(
        norm_gains.astype(F32), gains_moment.astype(F32), gains_square.astype(F32), mine[3:5], small_rate, 0.0
    )
    return (block_out[None], token_grad[None], *inner, *outer, *gate, *down, *conv, *gains)


def shifted(block, axis, distance):
    devices = range(lax.axis_size(axis))
    route = [(i - distance, i) for i in devices if i - distance in devices]
    return lax.ppermute(block, axis, route)


def norm_forward(values, gain_vector):
    norm_scale = lax.rsqrt(jnp.mean(values * values, axis=-1, keepdims=True) + norm_eps)
    unit_rows = values * norm_scale
    return (unit_rows, norm_scale, (unit_rows * gain_vector).astype(jnp.bfloat16))


def norm_backward(grad_normed, unit_rows, norm_scale, gain_vector):
    gain_grad = jnp.sum(grad_normed * unit_rows, axis=(0, 1))
    grad_unit = grad_normed * gain_vector
    grad_values = norm_scale * (
        grad_unit - unit_rows * jnp.mean(grad_unit * unit_rows, axis=-1, keepdims=True)
    )
    return (gain_grad, grad_values)


def plain_body(
    tokens,
    cotangent,
    in_proj,
    in_moment,
    in_square,
    out_proj,
    out_moment,
    out_square,
    gate_up,
    gate_moment,
    gate_square,
    down_proj,
    down_moment,
    down_square,
    conv_kernel,
    conv_moment,
    conv_square,
    norm_gains,
    gains_moment,
    gains_square,
):
    gathered = (
        lax.all_gather(in_proj, "shard", axis=0, tiled=True),
        lax.all_gather(out_proj, "shard", axis=0, tiled=True),
        lax.all_gather(gate_up, "shard", axis=1, tiled=True),
        lax.all_gather(down_proj, "shard", axis=1, tiled=True),
        lax.all_gather(conv_kernel, "shard", axis=1, tiled=True),
        lax.all_gather(norm_gains, "shard", axis=1, tiled=True),
    )
    full_in, full_out, full_gate, full_down, full_conv, full_gains = gathered
    gains_float = full_gains.astype(jnp.float32)
    conv_float = full_conv.astype(jnp.float32)
    inputs = tokens.astype(jnp.float32)
    model_width = inputs.shape[2]
    rows_count = inputs.shape[1]
    unit_one, scale_one, normed_one = norm_forward(inputs, gains_float[0])
    projected = jnp.einsum("scd,de->sce", normed_one, full_in, preferred_element_type=jnp.float32)
    first_gate = projected[:, :, :model_width]
    second_gate = projected[:, :, model_width : 2 * model_width]
    conv_input = projected[:, :, 2 * model_width :]
    mixed_in = (first_gate * conv_input).astype(jnp.bfloat16)
    before = shifted(mixed_in[:, rows_count - 2 :, :], "seq", 1)
    extended = jnp.concatenate([before, mixed_in], axis=1).astype(jnp.float32)
    convolved = (
        conv_float[0] * extended[:, :-2]
        + conv_float[1] * extended[:, 1:-1]
        + conv_float[2] * extended[:, 2:]
    )
    gated_out = (second_gate * convolved).astype(jnp.bfloat16)
    middle = inputs + jnp.einsum(
        "scd,de->sce", gated_out, full_out, preferred_element_type=jnp.float32
    )
    unit_two, scale_two, normed_two = norm_forward(middle, gains_float[1])
    gate_value = jnp.einsum(
        "scd,df->scf", normed_two, full_gate[0], preferred_element_type=jnp.float32
    )
    upward = jnp.einsum("scd,df->scf", normed_two, full_gate[1], preferred_element_type=jnp.float32)
    hidden = (jax.nn.silu(gate_value) * upward).astype(jnp.bfloat16)
    result = middle + jnp.einsum(
        "scf,fd->scd", hidden, full_down, preferred_element_type=jnp.float32
    )
    block_out = result.astype(jnp.bfloat16)
    regathered = (
        lax.all_gather(in_proj, "shard", axis=0, tiled=True),
        lax.all_gather(out_proj, "shard", axis=0, tiled=True),
        lax.all_gather(gate_up, "shard", axis=1, tiled=True),
        lax.all_gather(down_proj, "shard", axis=1, tiled=True),
        lax.all_gather(conv_kernel, "shard", axis=1, tiled=True),
        lax.all_gather(norm_gains, "shard", axis=1, tiled=True),
    )
    full_in, full_out, full_gate, full_down, full_conv, full_gains = regathered
    gains_float = full_gains.astype(jnp.float32)
    conv_float = full_conv.astype(jnp.float32)
    grad_result = cotangent.astype(jnp.float32)
    grad_hidden = jnp.einsum(
        "scd,fd->scf", cotangent, full_down, preferred_element_type=jnp.float32
    )
    grad_down = jnp.einsum("scf,scd->fd", hidden, cotangent, preferred_element_type=jnp.float32)
    sigmoid_gate = jax.nn.sigmoid(gate_value)
    grad_gate = (
        grad_hidden * upward * sigmoid_gate * (1.0 + gate_value * (1.0 - sigmoid_gate))
    ).astype(jnp.bfloat16)
    grad_upward = (grad_hidden * jax.nn.silu(gate_value)).astype(jnp.bfloat16)
    grad_gate_up = jnp.stack(
        [
            jnp.einsum("scd,scf->df", normed_two, grad_gate, preferred_element_type=jnp.float32),
            jnp.einsum("scd,scf->df", normed_two, grad_upward, preferred_element_type=jnp.float32),
        ]
    )
    grad_normed_two = jnp.einsum(
        "scf,df->scd", grad_gate, full_gate[0], preferred_element_type=jnp.float32
    ) + jnp.einsum("scf,df->scd", grad_upward, full_gate[1], preferred_element_type=jnp.float32)
    gain_two, grad_from_two = norm_backward(grad_normed_two, unit_two, scale_two, gains_float[1])
    grad_middle = grad_result + grad_from_two
    middle_low = grad_middle.astype(jnp.bfloat16)
    grad_out = jnp.einsum("scd,sce->de", gated_out, middle_low, preferred_element_type=jnp.float32)
    grad_gated = jnp.einsum("sce,de->scd", middle_low, full_out, preferred_element_type=jnp.float32)
    grad_second = grad_gated * convolved
    grad_conv_out = grad_gated * second_gate
    grad_conv = jnp.stack(
        [
            jnp.sum(grad_conv_out * extended[:, offset : offset + rows_count], axis=(0, 1))
            for offset in range(3)
        ]
    )
    grad_extended = (
        jnp.pad(grad_conv_out * conv_float[0], ((0, 0), (0, 2), (0, 0)))
        + jnp.pad(grad_conv_out * conv_float[1], ((0, 0), (1, 1), (0, 0)))
        + jnp.pad(grad_conv_out * conv_float[2], ((0, 0), (2, 0), (0, 0)))
    )
    from_next = shifted(grad_extended[:, :2, :], "seq", -1)
    grad_mixed = grad_extended[:, 2:, :] + jnp.pad(from_next, ((0, 0), (rows_count - 2, 0), (0, 0)))
    grad_projected = jnp.concatenate(
        [grad_mixed * conv_input, grad_second, grad_mixed * first_gate], axis=2
    ).astype(jnp.bfloat16)
    grad_in = jnp.einsum(
        "scd,sce->de", normed_one, grad_projected, preferred_element_type=jnp.float32
    )
    grad_normed_one = jnp.einsum(
        "sce,de->scd", grad_projected, full_in, preferred_element_type=jnp.float32
    )
    gain_one, grad_from_one = norm_backward(grad_normed_one, unit_one, scale_one, gains_float[0])
    token_grad = (grad_middle + grad_from_one).astype(jnp.bfloat16)
    grad_gains = jnp.stack([gain_one, gain_two])
    parts = (
        lax.psum_scatter(grad_in, "shard", scatter_dimension=0, tiled=True),
        lax.psum_scatter(grad_out, "shard", scatter_dimension=0, tiled=True),
        lax.psum_scatter(grad_gate_up, "shard", scatter_dimension=1, tiled=True),
        lax.psum_scatter(grad_down, "shard", scatter_dimension=1, tiled=True),
        lax.psum_scatter(grad_conv, "shard", scatter_dimension=1, tiled=True),
        lax.psum_scatter(grad_gains, "shard", scatter_dimension=1, tiled=True),
    )
    totals = lax.psum((parts[0], parts[1], parts[2], parts[3], parts[4], parts[5]), ("rep", "seq"))
    matrix_rate = 2.0 * model_width ** (-0.5)
    down_rate = 2.0 * gate_up.shape[2] ** (-0.5)
    in_next, in_moment_next, in_square_next = adamw(
        in_proj.astype(jnp.float32),
        in_moment.astype(jnp.float32),
        in_square.astype(jnp.float32),
        totals[0],
        matrix_rate,
        decay_rate,
    )
    out_next, out_moment_next, out_square_next = adamw(
        out_proj.astype(jnp.float32),
        out_moment.astype(jnp.float32),
        out_square.astype(jnp.float32),
        totals[1],
        matrix_rate,
        decay_rate,
    )
    gate_next, gate_moment_next, gate_square_next = adamw(
        gate_up.astype(jnp.float32),
        gate_moment.astype(jnp.float32),
        gate_square.astype(jnp.float32),
        totals[2],
        matrix_rate,
        decay_rate,
    )
    down_next, down_moment_next, down_square_next = adamw(
        down_proj.astype(jnp.float32),
        down_moment.astype(jnp.float32),
        down_square.astype(jnp.float32),
        totals[3],
        down_rate,
        decay_rate,
    )
    conv_next, conv_moment_next, conv_square_next = adamw(
        conv_kernel.astype(jnp.float32),
        conv_moment.astype(jnp.float32),
        conv_square.astype(jnp.float32),
        totals[4],
        small_rate,
        0.0,
    )
    gains_next, gains_moment_next, gains_square_next = adamw(
        norm_gains.astype(jnp.float32),
        gains_moment.astype(jnp.float32),
        gains_square.astype(jnp.float32),
        totals[5],
        small_rate,
        0.0,
    )
    return (
        block_out,
        token_grad,
        in_next,
        in_moment_next,
        in_square_next,
        out_next,
        out_moment_next,
        out_square_next,
        gate_next,
        gate_moment_next,
        gate_square_next,
        down_next,
        down_moment_next,
        down_square_next,
        conv_next,
        conv_moment_next,
        conv_square_next,
        gains_next,
        gains_moment_next,
        gains_square_next,
    )


def solution(mesh):
    act = P(("rep", "shard"), "seq", None)
    weights = (
        (P("shard", None),) * 6 + (P(None, "shard", None),) * 3 + (P(None, "shard"),) * 9
    )
    specs = (act, act) + weights
    sizes = (mesh.shape["rep"], mesh.shape["seq"], mesh.shape["shard"])
    body = fused_body if sizes == (4, 4, 2) else plain_body
    return jax.shard_map(body, mesh=mesh, in_specs=specs, out_specs=specs, check_vma=False)
```

```python
import functools

import jax
import jax.numpy as jnp
from jax import lax
from jax.experimental import pallas as pl
from jax.experimental.pallas import tpu as pltpu
from jax.sharding import PartitionSpec as P

STEP = 10
norm_eps = 1e-05
beta_one = 0.9
beta_two = 0.95
adam_eps = 1e-08
decay_rate = 0.1
small_rate = 0.4

BF = jnp.bfloat16
F32 = jnp.float32
MESH = pl.DeviceIdType.MESH
GROUPS = 3
CHUNK = 128
TILE = 16
PLAN = (
    (0, 0, 0, 0, 1),
    (0, 0, 0, 0, 2),
    (0, 0, 0, 1, 3),
    (0, 0, 1, 3, 5),
    (0, 0, 2, 4, 6),
    (0, 1, 3, 5, 8),
    (0, 2, 4, 6, 10),
    (0, 4, 6, 8, 11),
    (0, 10, 13, 16, 20),
    (4, 13, 16, 18, 23),
    (8, 15, 18, 20, 25),
    (13, 19, 22, 24, 28),
    (17, 23, 26, 28, 31),
)
HELD = 40

SLOTS = 64
SPOTS = 16


def dot(a, b):
    return lax.dot_general(a, b, (((1,), (0,)), ((), ())), preferred_element_type=F32)


def dot_nt(a, b):
    return lax.dot_general(a, b, (((1,), (1,)), ((), ())), preferred_element_type=F32)


def dot_tn(a, b):
    return lax.dot_general(a, b, (((0,), (0,)), ((), ())), preferred_element_type=F32)


def block_kernel(
    dims,
    tok_h, cot_h, in_h, out_h, gu_h, dn_h, small_h,
    block_out, token_grad, grads, mine, other, small_grads,
    WG, WD, WIN, WOUT, SM, TOK, N1, N2, CT, ML,
    PROJ, MX, CONV, GATED, GCO, ACT, HID, FA, FB, GS, GO, RX,
    MID, GM, P32, SC, RC, SY, RY, SG,
    ss, rs, ls, xs, xr, z1s, z1r, z2s, z2r, ts, tr, ys, yr, c1s, c1r, c2s, c2r, gl,
    ready_w, ready_a,
):
    D, T, FQ, F = dims
    H, Q, R, FG = D // 2, FQ // 2, 4 * T, F // GROUPS
    MT = H // 2
    GR = H + H // 2
    NCH = 2 * (GROUPS + 1) * GR // CHUNK
    PER = 2 * GR // CHUNK
    NGU = 2 * H // CHUNK
    z = lax.axis_index("rep")
    s = lax.axis_index("seq")
    x = lax.axis_index("shard")
    y, c = s // 2, s % 2
    h = z % 2
    is_mid = jnp.logical_and(z > 0, z < 3)
    is_end = jnp.logical_or(z == 0, z == 3)
    xo = 1 - x
    xp = (z, s, xo)
    cp = (z, 2 * y + 1 - c, x)
    yp = (z, 2 * (1 - y) + c, x)
    zp = (z + 1 - 2 * h, s, x)
    mp = (3 - z, s, x)

    def block(i):
        return 2 * (y + (i // 2) * (1 - 2 * y)) + c + (i % 2) * (1 - 2 * c)

    def at(start, size, unit):
        return pl.ds(pl.multiple_of(start, unit), size)

    def rows(m, n=T):
        return at(m * n, n, n)

    slots, spots = {}, {}

    def remote(name, src, dst, dev):
        k = slots.setdefault(name, len(slots))
        return pltpu.make_async_remote_copy(
            src_ref=src, dst_ref=dst, send_sem=ss.at[k], recv_sem=rs.at[k], device_id=dev, device_id_type=MESH
        )

    def local(name, src, dst):
        return pltpu.make_async_copy(src, dst, ls.at[spots.setdefault(name, len(spots))])

    barrier = pltpu.get_barrier_semaphore()
    for dev in (xp, cp, yp, zp):
        pl.semaphore_signal(barrier, inc=1, device_id=dev, device_id_type=MESH)

    @pl.when(is_mid)
    def _():
        pl.semaphore_signal(barrier, inc=1, device_id=mp, device_id_type=MESH)

    def weight(name, owner, half=None):
        kind, p = name.split("_")
        p = int(p)
        if half is None:
            half, parts = 0, 1
        else:
            parts = 2
        n = H // parts
        if kind == "in":
            return WIN.at[at(H * owner + n * half, n, n), FQ * p : FQ * (p + 1)]
        if kind == "out":
            n = Q // parts
            return WOUT.at[at(Q * owner + n * half, n, n)]
        if kind == "down":
            n = FG // parts
            return WD.at[at(FG * p + n * half, n, n), at(H * owner, H, H)]
        j = 0 if kind == "gate" else 1
        return WG.at[at(GR + D * p + H * owner + n * half, n, H // 2), FG * j : FG * (j + 1)]

    def weight_source(name, half=None):
        kind, p = name.split("_")
        p = int(p)
        parts = 1 if half is None else 2
        first = 0 if half is None else half
        n = H // parts
        if kind == "in":
            dst = at(H * x + n * first, n, n)
            return [
                (in_h.at[at(n * first, n, n), at(D * p + H * k + Q * s, Q, Q)], WIN.at[dst, pl.ds(FQ * p + Q * k, Q)])
                for k in range(2)
            ]
        dst = weight(name, x, half)
        if kind == "out":
            n = Q // parts
            return [(out_h.at[at(Q * s + n * first, n, n)], dst)]
        if kind == "down":
            n = FG // parts
            return [(dn_h.at[at(F * s + FG * p + n * first, n, n)], dst)]
        j = 0 if kind == "gate" else 1
        return [(gu_h.at[j, at(n * first, n, n), at(F * s + FG * p, FG, FG)], dst)]

    loads = [
        local("tok", tok_h, TOK),
        local("small", small_h, SM.at[x]),
        local("ct", cot_h, CT.at[rows(s)]),
    ]
    order = ["in_0", "in_1", "in_2", "out_0"]
    for g in range(GROUPS):
        order += ["gate_%d" % g, "up_%d" % g, "down_%d" % g]
    for name in order:
        for src, dst in weight_source(name):
            loads.append(local("in" if name[:3] == "in_" else name.replace("out_0", "out"), src, dst))
    for copy in loads:
        copy.start()

    def local_wait(name):
        if name == "tok":
            copy = local(name, tok_h, TOK)
        elif name == "small":
            copy = local(name, small_h, SM.at[x])
        elif name == "ct":
            copy = local(name, cot_h, CT.at[rows(s)])
        elif name == "in":
            copy = local(name, WIN.at[rows(x, H)], WIN.at[rows(x, H)])
        else:
            here = weight(name if name != "out" else "out_0", x)
            copy = local(name, here, here)
        copy.wait()

    @pl.when(is_mid)
    def _():
        pl.semaphore_wait(barrier, 5)

    @pl.when(is_end)
    def _():
        pl.semaphore_wait(barrier, 4)

    def weight_pass(name):
        here = weight(name, xo, h)
        remote(name, here, here, xp).wait_recv()
        remote(name + "_z", here, here, zp).start()

    def weight_wait(name):
        there = weight(name, xo, 1 - h)
        remote(name + "_z", there, there, zp).wait_recv()

    def weight_passed(name):
        here = weight(name, xo, h)
        remote(name + "_z", here, here, zp).wait_send()

    def group_wait(g):
        for kind in ("gate_", "up_", "down_"):
            local_wait(kind + str(g))
            weight_wait(kind + str(g))

    def gather_copy(name, buf, kind, src=None):
        m = block(2) if kind == "f" else s
        return remote(
            name + "_" + kind, buf.at[rows(m)] if src is None else src, buf.at[rows(m)], yp if kind == "y" else cp
        )

    def gather_start(name, buf):
        gather_copy(name, buf, "y").start()
        gather_copy(name, buf, "c").start()

    def gather_step(name, buf, i, between=None):
        @pl.when(i == 1)
        def _():
            remote(name + "_c", buf.at[rows(block(1))], buf.at[rows(block(1))], cp).wait_recv()

        @pl.when(i == 2)
        def _():
            remote(name + "_y", buf.at[rows(block(2))], buf.at[rows(block(2))], yp).wait_recv()
            if between is not None:
                between()
            gather_copy(name, buf, "f").start()

        @pl.when(i == 3)
        def _():
            remote(name + "_f", buf.at[rows(block(3))], buf.at[rows(block(3))], cp).wait_recv()

    remote("small", small_h, SM.at[x], xp).start()
    gather_copy("n1", N1, "y", tok_h).start()
    gather_copy("ct", CT, "y", cot_h).start()
    gather_copy("ct", CT, "c", cot_h).start()
    for name in order:
        for src, dst in weight_source(name, h):
            remote(name, src, dst, xp).start()

    def sum_core(name, lot, k):
        return remote(name + "_" + str(k), SC.at[lot, k], RC.at[lot, k], cp)

    def sum_y(name, lot):
        return remote(name + "_y", SY.at[lot], RY.at[lot], yp)

    def sum_emit(name, lot, i, partial):
        @pl.when(i % 2 == 0)
        def _():
            P32[i // 2] = partial

        @pl.when(i == 1)
        def _():
            SC[lot, 1] = partial.astype(BF)
            sum_core(name, lot, 1).start()

        @pl.when(i == 3)
        def _():
            SC[lot, 0] = partial.astype(BF)
            sum_core(name, lot, 0).start()

    def sum_cross(name, lot):
        sum_core(name, lot, 0).wait_recv()

        def add(r):
            SY[lot, r] = (P32[1, r] + RC[lot, 0, r].astype(F32)).astype(BF)

        tiles(T, add, 32)
        sum_y(name, lot).start()

    def sum_wait(name, lot):
        sum_core(name, lot, 1).wait_recv()
        sum_y(name, lot).wait_recv()

    def sum_rows(lot, r):
        return P32[0, r] + RC[lot, 1, r].astype(F32) + RY[lot, r].astype(F32)

    def sum_done(name, lot):
        sum_core(name, lot, 0).wait_send()
        sum_core(name, lot, 1).wait_send()
        sum_y(name, lot).wait_send()

    def tiles(n, body, size=TILE):
        def step(t, carry):
            body(pl.ds(pl.multiple_of(t * size, size), size))
            return carry

        lax.fori_loop(0, n // size, step, 0)

    def blocks(body, order=(0, 1, 2, 3)):
        first, step = order[0], order[1] - order[0]

        def turn(t, carry):
            i = first + step * t
            body(i, block(i))
            return carry

        lax.fori_loop(0, len(order), turn, 0)

    def gain(k):
        return jnp.concatenate([SM[0, 3 + k : 4 + k, :], SM[1, 3 + k : 4 + k, :]], axis=1)

    def tap(k):
        cols = rows(s, Q)
        return jnp.concatenate([SM[0, k : k + 1, cols], SM[1, k : k + 1, cols]], axis=1)

    local_wait("tok")
    local_wait("small")
    remote("small", small_h, SM.at[xo], xp).wait()
    SG[0] = jnp.zeros_like(SG[0])
    MX[0:8] = jnp.zeros((8, FQ), F32)
    GCO[R : R + 8] = jnp.zeros((8, FQ), F32)
    gain_one = gain(0)

    def norm_one(src, first, m):
        def one(r):
            v = src[at(first + r.start, 32, 32)].astype(F32)
            scale = lax.rsqrt(jnp.mean(v * v, axis=-1, keepdims=True) + norm_eps)
            N1[at(m * T + r.start, 32, 32)] = (v * scale * gain_one).astype(BF)

        tiles(T, one, 32)

    norm_one(TOK, 0, s)
    gather_copy("n1", N1, "c").start()

    for name in order[:3]:
        weight_pass(name)
    local_wait("in")
    for name in order[:3]:
        weight_wait(name)
    weight_pass("out_0")

    def project(i, m):
        gather_step("n1", N1, i, lambda: norm_one(N1, block(2) * T, block(2)))
        p = dot(N1[rows(m)], WIN[...])
        PROJ[rows(m)] = p
        mixed = (p[:, :FQ] * p[:, 2 * FQ :]).astype(BF)
        MX[at(8 + m * T, T, 8)] = mixed.astype(F32)

    blocks(project)
    weight_pass("gate_0")
    local_wait("out")
    weight_wait("out_0")

    def convolve(i, m):
        ext = MX[at(m * T, T + 8, 8)]
        conv = tap(0) * ext[6 : 6 + T] + tap(1) * ext[7 : 7 + T] + tap(2) * ext[8 : 8 + T]
        CONV[rows(m)] = conv
        gated = (PROJ[rows(m), FQ : 2 * FQ] * conv).astype(BF)
        GATED[rows(m)] = gated
        sum_emit("ro", 0, i, dot(gated, WOUT[...]))

    blocks(convolve, (3, 2))
    weight_pass("up_0")
    sum_cross("ro", 0)
    blocks(convolve, (1, 0))
    for name in ("down_0", "gate_1", "up_1"):
        weight_pass(name)
    sum_wait("ro", 0)

    gain_two = gain(1)

    def norm_two(r):
        v = TOK[r].astype(F32) + sum_rows(0, r)
        MID[r] = v
        scale = lax.rsqrt(jnp.mean(v * v, axis=-1, keepdims=True) + norm_eps)
        N2[at(s * T + r.start, 32, 32)] = (v * scale * gain_two).astype(BF)

    tiles(T, norm_two, 32)
    gather_start("n2", N2)
    sum_done("ro", 0)
    weight_pass("down_1")

    def feed(g):
        def unit(i, m):
            if g == 0:
                gather_step("n2", N2, i)
                gather_step("ct", CT, i)
            FA[...] = dot(N2[rows(m)], WG[GR + D * g : GR + D * (g + 1)])
            FB[...] = dot_nt(CT[rows(m)], WD[FG * g : FG * (g + 1)])

            def act(r):
                gate, up, gh = FA[r, 0:FG], FA[r, FG:], FB[r]
                sig = jax.nn.sigmoid(gate)
                silu = gate * sig
                ro = at(GR + R * g + m * T + r.start, 32, 32)
                ACT[ro, 0:FG] = (gh * up * sig * (1.0 + gate * (1.0 - sig))).astype(BF)
                ACT[ro, FG:] = (gh * silu).astype(BF)
                HID[at(m * T + r.start, 32, 32), FG * g : FG * (g + 1)] = (silu * up).astype(BF)

            tiles(T, act, 32)

        return unit

    def group_grad(g, dst, owner):
        base = GR * g

        def step(t, carry):
            lhs = N2[:, at(H * owner + MT * t, MT, MT)]
            dst[at(base + MT * t, MT, MT)] = dot_tn(lhs, ACT[GR + R * g : GR + R * (g + 1)]).astype(BF)
            lhs = CT[:, at(H * owner + MT * t, MT, MT)]
            low = dot_tn(lhs, HID[:, FG * g : FG * (g + 1)]).astype(BF)
            for j in range(2):
                dst[at(base + H + CHUNK * t, CHUNK, CHUNK), FG * j : FG * (j + 1)] = low[CHUNK * j : CHUNK * (j + 1)]
            return carry

        lax.fori_loop(0, H // MT, step, 0)

    def chunk(ref, k):
        return ref.at[rows(k // 2, CHUNK), at(FG * (k % 2), FG, FG)]

    def step_copy(src, dst, send, recv, k, dev):
        return pltpu.make_async_remote_copy(
            src_ref=src, dst_ref=dst, send_sem=send.at[k], recv_sem=recv.at[k], device_id=dev, device_id_type=MESH
        )

    def x_copy(k):
        return step_copy(chunk(GS, k), chunk(RX, k), xs, xr, k, xp)

    def z1_copy(k):
        return step_copy(chunk(GO, k), chunk(WG, k), z1s, z1r, k, zp)

    def z2_copy(k):
        return step_copy(chunk(RX, k), chunk(ACT, k), z2s, z2r, k, mp)

    def t_copy(k):
        return step_copy(chunk(GO, k), chunk(WG, k), ts, tr, k, zp)

    def is_wide(k):
        return jnp.logical_and(k < GROUPS * PER, k % PER < NGU)

    def wide_at(k, m):
        return grads.at[m, rows((NGU // 2) * (k // PER) + (k % PER) // 2, CHUNK), at(FG * (k % 2), FG, FG)]

    def late_at(k, ref, inner):
        if inner:
            row = ((PER - NGU) // 2) * GROUPS + (k - GROUPS * PER) // 2
        else:
            row = ((PER - NGU) // 2) * (k // PER) + (k % PER - NGU) // 2
        return ref.at[rows(row, CHUNK), at(FG * (k % 2), FG, FG)]

    def y_copy(k, src):
        return step_copy(chunk(src, k), wide_at(k, s), ys, yr, k, yp)

    def c2_copy(k):
        m = block(2)
        return step_copy(wide_at(k, m), wide_at(k, m), c2s, c2r, k, cp)

    def spread(k, src):
        @pl.when(is_wide(k))
        def _():
            y_copy(k, src).start()
            step_copy(chunk(src, k), wide_at(k, s), c1s, c1r, k, cp).start()
            pltpu.make_async_copy(chunk(src, k), wide_at(k, s), gl.at[k]).start()

        for inner in (False, True):
            if inner:
                cond = k >= GROUPS * PER
            else:
                cond = jnp.logical_and(k < GROUPS * PER, k % PER >= NGU)

            @pl.when(cond)
            def _():
                step_copy(chunk(src, k), late_at(k, other, inner), c1s, c1r, k, cp).start()
                pltpu.make_async_copy(chunk(src, k), late_at(k, mine, inner), gl.at[k]).start()

    def add(k, dst, one, two):
        total = chunk(one, k)[...].astype(F32) + chunk(two, k)[...].astype(F32)
        chunk(dst, k)[...] = total.astype(BF)

    def add_x(k):
        x_copy(k).wait_recv()
        add(k, GO, GO, RX)
        pl.when(is_end)(lambda: z1_copy(k).start())

    def add_end(k):
        @pl.when(is_mid)
        def _():
            z1_copy(k).wait_recv()
            add(k, RX, GO, WG)
            z2_copy(k).start()

    def add_mid(k):
        @pl.when(is_mid)
        def _():
            z2_copy(k).wait_recv()
            add(k, GO, RX, ACT)
            t_copy(k).start()
            spread(k, GO)

    def take(k):
        @pl.when(is_end)
        def _():
            t_copy(k).wait_recv()
            spread(k, WG)

    def hand(k):
        @pl.when(is_wide(k))
        def _():
            m = block(2)
            step_copy(wide_at(k, m), wide_at(k, m), ys, yr, k, yp).wait_recv()
            c2_copy(k).start()

    stages = (hand, take, add_mid, add_end, add_x)
    place = [0] * len(stages)

    def advance(*goals, late=True):
        first = tuple(place)
        n = max(goal - at for goal, at in zip(goals, first))

        def step(t, carry):
            for body, at, goal in zip(stages, first, goals):
                if goal > at:
                    skip = n - (goal - at) if late else 0
                    pl.when(jnp.logical_and(t >= skip, t < skip + goal - at))(functools.partial(body, at + t - skip))
            return carry

        lax.fori_loop(0, n, step, 0)
        place[:] = goals

    def send(first, last):
        def step(k, carry):
            x_copy(k).start()
            return carry

        lax.fori_loop(first, last, step, 0)

    local_wait("ct")
    group_wait(0)
    blocks(feed(0), (0, 1))
    weight_pass("gate_2")
    group_wait(1)
    weight_pass("up_2")
    blocks(feed(1), (0, 1))
    blocks(feed(0), (2, 3))
    group_grad(0, GS, xo)
    send(0, PER)
    weight_pass("down_2")
    group_grad(0, GO, x)
    advance(*PLAN[0])
    blocks(feed(1), (2, 3))
    advance(*PLAN[1])
    group_grad(1, GS, xo)
    send(PER, 2 * PER)
    advance(*PLAN[2])
    group_wait(2)
    blocks(feed(2), (0, 1, 2, 3))
    advance(*PLAN[3])
    group_grad(2, GS, xo)
    send(2 * PER, 3 * PER)
    advance(*PLAN[4])

    def back_feed(i, m):
        partial = dot_nt(ACT[at(GR + m * T, T, T)], WG[GR : GR + D])
        for g in range(1, GROUPS):
            partial = partial + dot_nt(ACT[at(GR + R * g + m * T, T, T)], WG[GR + D * g : GR + D * (g + 1)])
        sum_emit("rg", 1, i, partial)

    blocks(back_feed, (3, 2))
    sum_cross("rg", 1)
    advance(*PLAN[5])
    blocks(back_feed, (1, 0))
    for g in range(GROUPS):
        weight_passed("gate_%d" % g)
        weight_passed("up_%d" % g)
    pl.semaphore_signal(ready_w, inc=1, device_id=zp, device_id_type=MESH)
    group_grad(1, GO, x)
    advance(*PLAN[6])
    group_grad(2, GO, x)

    @pl.when(is_mid)
    def _():
        pl.semaphore_signal(ready_a, inc=1, device_id=mp, device_id_type=MESH)

    pl.semaphore_wait(ready_w, 1)

    @pl.when(is_mid)
    def _():
        pl.semaphore_wait(ready_a, 1)

    advance(*PLAN[7])

    sum_wait("rg", 1)

    def back_two(t, acc):
        r = at(t * TILE, TILE, TILE)
        v = MID[r]
        scale = lax.rsqrt(jnp.mean(v * v, axis=-1, keepdims=True) + norm_eps)
        unit = v * scale
        e = sum_rows(1, r)
        eu = e * unit
        ew = e * gain_two
        grad = scale * (ew - unit * jnp.mean(ew * unit, axis=-1, keepdims=True))
        ro = at(s * T + t * TILE, TILE, TILE)
        gm = CT[ro].astype(F32) + grad
        GM[r] = gm
        ML[ro] = gm.astype(BF)
        return acc + jnp.sum(eu, axis=0, keepdims=True)

    SG[0, 4:5, :] = lax.fori_loop(0, T // TILE, back_two, jnp.zeros((1, D), F32))
    gather_start("ml", ML)
    sum_done("rg", 1)
    advance(*PLAN[8])

    def gated_back(i, m):
        gather_step("ml", ML, i)
        gg = dot_nt(ML[rows(m)], WOUT[...])
        gco = gg * PROJ[rows(m), FQ : 2 * FQ]
        GCO[rows(m)] = gco
        PROJ[rows(m), FQ : 2 * FQ] = gg * CONV[rows(m)]

    blocks(gated_back)
    for kind in "cyf":
        gather_copy("n2", N2, kind).wait_send()

    def conv_back(t, acc):
        i = 3 - t
        m = block(i)
        gco = GCO[at(m * T, T + 8, 8)]
        ext = MX[at(m * T, T + 8, 8)]
        here = gco[0:T]
        gm = tap(2) * here + tap(1) * gco[1 : 1 + T] + tap(0) * gco[2 : 2 + T]
        p = PROJ[rows(m)]
        low = jnp.concatenate([gm * p[:, 2 * FQ :], p[:, FQ : 2 * FQ], gm * p[:, :FQ]], axis=1).astype(BF)
        N2[rows(m), 0 : 3 * FQ] = low
        sum_emit("ri", 1, i, dot_nt(low, WIN[...]))
        return tuple(
            a + jnp.sum(here * ext[6 + k : 6 + k + T], axis=0, keepdims=True) for k, a in enumerate(acc)
        )

    conv_grads = lax.fori_loop(0, 4, conv_back, (jnp.zeros((1, FQ), F32),) * 3)
    for k in range(3):
        SG[0, k : k + 1, rows(s, Q)] = conv_grads[k][:, :Q]
        SG[0, k : k + 1, at(H + s * Q, Q, Q)] = conv_grads[k][:, Q:]
    sum_cross("ri", 1)

    def io_grad(dst, owner):
        base = GROUPS * GR

        def step(t, carry):
            lhs = N1[:, at(H * owner + MT * t, MT, MT)]
            dst[at(base + MT * t, MT, MT)] = dot_tn(lhs, N2[:, 0 : 3 * FQ]).astype(BF)
            right = GATED[:, rows(owner, Q)]
            for j in range(2):
                lhs = ML[:, at(H * j + MT * t, MT, MT)]
                low = dot_tn(lhs, right).astype(BF)
                for k in range(2):
                    dst[at(base + H + CHUNK * t, CHUNK, CHUNK), FG * k + Q * j : FG * k + Q * (j + 1)] = low[
                        CHUNK * k : CHUNK * (k + 1)
                    ]
            for k in range(2):
                dst[at(base + H + CHUNK * t, CHUNK, CHUNK), FG * k + 2 * Q : FG * (k + 1)] = jnp.zeros(
                    (CHUNK, FG - 2 * Q), BF
                )
            return carry

        lax.fori_loop(0, H // MT, step, 0)

    io_grad(GS, xo)
    send(GROUPS * PER, HELD)
    advance(*PLAN[9])
    io_grad(GO, x)
    advance(*PLAN[10])

    sum_wait("ri", 1)
    low_out = SC.at[0, 0]

    def back_one(t, acc):
        r = at(t * TILE, TILE, TILE)
        v = TOK[r].astype(F32)
        scale = lax.rsqrt(jnp.mean(v * v, axis=-1, keepdims=True) + norm_eps)
        unit = v * scale
        e = sum_rows(1, r)
        eu = e * unit
        ew = e * gain_one
        grad = scale * (ew - unit * jnp.mean(ew * unit, axis=-1, keepdims=True))
        low_out[r] = (GM[r] + grad).astype(BF)
        return acc + jnp.sum(eu, axis=0, keepdims=True)

    SG[0, 3:4, :] = lax.fori_loop(0, T // TILE, back_one, jnp.zeros((1, D), F32))
    out_copy = pltpu.make_async_copy(low_out, token_grad, ls.at[spots["tok"]])
    out_copy.start()
    sum_done("ri", 1)

    def small_start(name, dev, k):
        remote(name, SG.at[0], SG.at[k], dev).start()

    def small_end(name, dev, k):
        remote(name, SG.at[0], SG.at[k], dev).wait()
        SG[0] = SG[0] + SG[k]

    small_start("sg_c", cp, 2)
    advance(*PLAN[11])
    small_end("sg_c", cp, 2)
    small_start("sg_y", yp, 3)
    out_copy.wait()

    def down(i, m):
        sum_emit("rr", 0, i, dot(HID[rows(m)], WD[...]))

    blocks(down, (3, 2, 1, 0))
    sum_cross("rr", 0)
    small_end("sg_y", yp, 3)
    small_start("sg_x", xp, 1)
    send(HELD, NCH)
    advance(*PLAN[12])

    def on(first, last):
        for k in range(first, last + 1, 2):
            advance(*(min(max(k - lag, at), NCH) for lag, at in zip((12, 9, 6, 3, 0), place)))

    on(32, 38)
    sum_wait("rr", 0)
    sum_done("rr", 0)

    def result(r):
        low_out[r] = (MID[r] + sum_rows(0, r)).astype(BF)

    tiles(T, result, 32)
    out_copy = pltpu.make_async_copy(low_out, block_out, ls.at[spots["tok"]])
    out_copy.start()
    on(40, 42)
    small_end("sg_x", xp, 1)
    pl.when(is_end)(lambda: small_start("sg_a", zp, 4))
    on(44, 46)

    @pl.when(is_end)
    def _():
        remote("sg_a", SG.at[0], SG.at[4], zp).wait_send()

    @pl.when(is_mid)
    def _():
        remote("sg_a", SG.at[0], SG.at[4], zp).wait_recv()
        SG[0] = SG[0] + SG[4]
        small_start("sg_b", mp, 5)

    on(48, 48)

    @pl.when(is_mid)
    def _():
        remote("sg_b", SG.at[0], SG.at[5], mp).wait()
        SG[6] = SG[0] + SG[5]
        remote("sg_t", SG.at[6], SG.at[6], zp).start()

    advance(*(NCH,) * 5, late=False)

    @pl.when(is_mid)
    def _():
        remote("sg_t", SG.at[6], SG.at[6], zp).wait_send()

    @pl.when(is_end)
    def _():
        remote("sg_t", SG.at[6], SG.at[6], zp).wait_recv()

    small_copy = pltpu.make_async_copy(SG.at[6], small_grads, ls.at[spots["small"]])
    small_copy.start()

    def finish(k, carry):
        x_copy(k).wait_send()

        @pl.when(is_end)
        def _():
            z1_copy(k).wait_send()

        @pl.when(is_mid)
        def _():
            z2_copy(k).wait_send()
            t_copy(k).wait_send()

        @pl.when(is_wide(k))
        def _():
            y_copy(k, GO).wait_send()
            c2_copy(k).wait()

        here = chunk(GO, k)
        step_copy(here, here, c1s, c1r, k, cp).wait()
        pltpu.make_async_copy(here, here, gl.at[k]).wait()
        return carry

    lax.fori_loop(0, NCH, finish, 0)
    out_copy.wait()
    small_copy.wait()
    for name in order:
        here = weight(name, x, h)
        remote(name, here, here, xp).wait_send()
        if name[0] not in "gu":
            weight_passed(name)
    for name, buf in (("n1", N1), ("ct", CT), ("ml", ML)):
        for kind in "cyf":
            gather_copy(name, buf, kind).wait_send()


def run_block(tokens, cotangent, in_proj, out_proj, gate_up, down_proj, small):
    T, D = tokens.shape
    F = gate_up.shape[2] // 4
    FQ = D // 4
    R = 4 * T
    H = D // 2
    W2 = 2 * F // GROUPS
    GR = H + H // 2
    NR = (GROUPS + 1) * GR
    dims = (D, T, FQ, F)
    NCH = 2 * NR // CHUNK
    hbm = pl.BlockSpec(memory_space=pltpu.HBM)
    dma = pltpu.SemaphoreType.DMA
    vmem = pltpu.VMEM
    late = jax.ShapeDtypeStruct((GROUPS * H // 2 + GR, W2), BF)
    scratch = [
        vmem((GR + NR, W2), BF),
        vmem((F, D), BF),
        vmem((D, 3 * FQ), BF),
        vmem((FQ, D), BF),
        vmem((2, 8, H), F32),
        vmem((T, D), BF),
        vmem((R, D), BF),
        vmem((R, D), BF),
        vmem((R, D), BF),
        vmem((R, D), BF),
        vmem((R, 3 * FQ), F32),
        vmem((R + 8, FQ), F32),
        vmem((R, FQ), F32),
        vmem((R, FQ), BF),
        vmem((R + 8, FQ), F32),
        vmem((GR + NR, W2), BF),
        vmem((R, F), BF),
        vmem((T, W2), F32),
        vmem((T, W2 // 2), F32),
        vmem((NR, W2), BF),
        vmem((NR, W2), BF),
        vmem((NR, W2), BF),
        vmem((T, D), F32),
        vmem((T, D), F32),
        vmem((2, T, D), F32),
        vmem((2, 2, T, D), BF),
        vmem((2, 2, T, D), BF),
        vmem((2, T, D), BF),
        vmem((2, T, D), BF),
        vmem((7, 8, D), F32),
        dma((SLOTS,)),
        dma((SLOTS,)),
        dma((SPOTS,)),
    ]
    scratch += [dma((NCH,))] * 15
    scratch += [pltpu.SemaphoreType.REGULAR, pltpu.SemaphoreType.REGULAR]
    flops = 6 * R * D * (3 * F + 4 * FQ) * 2
    return pl.pallas_call(
        functools.partial(block_kernel, dims),
        out_shape=(
            jax.ShapeDtypeStruct((T, D), BF),
            jax.ShapeDtypeStruct((T, D), BF),
            jax.ShapeDtypeStruct((4, GROUPS * H, W2), BF),
            late,
            late,
            jax.ShapeDtypeStruct((8, D), F32),
        ),
        in_specs=[hbm] * 7,
        out_specs=(hbm,) * 6,
        scratch_shapes=scratch,
        compiler_params=pltpu.CompilerParams(
            collective_id=0, has_side_effects=True, vmem_limit_bytes=62 * 2**20
        ),
        cost_estimate=pl.CostEstimate(flops=flops, bytes_accessed=60 * 2**20, transcendentals=R * F),
        name="block_kernel",
    )(tokens, cotangent, in_proj, out_proj, gate_up, down_proj, small)


def adamw(weight, first_moment, second_moment, gradient, step_rate, decay_factor):
    first_new = beta_one * first_moment + (1.0 - beta_one) * gradient
    second_new = beta_two * second_moment + (1.0 - beta_two) * gradient * gradient
    adam_ratio = (
        first_new
        / (1.0 - beta_one**STEP)
        / (jnp.sqrt(second_new / (1.0 - beta_two**STEP)) + adam_eps)
    )
    weight_new = weight - step_rate * (adam_ratio + decay_factor * weight)
    return (weight_new, first_new, second_new)


def update_values(rate, w, m, v, grad):
    w, m, v, grad = (a.astype(F32) for a in (w, m, v, grad))
    first = beta_one * m + (1.0 - beta_one) * grad
    second = beta_two * v + (1.0 - beta_two) * grad * grad
    u = second * (1.0 / (1.0 - beta_two**STEP))
    root = u * lax.rsqrt(u) + adam_eps
    return (1.0 - rate * decay_rate) * w - (rate / (1.0 - beta_one**STEP)) * first / root, first, second


def update_gate(rate, where, w, m, v, *refs):
    grads, new = refs[:GROUPS], refs[GROUPS:]
    FG = w.shape[2] // GROUPS
    for g in range(GROUPS):
        cols = slice(FG * g, FG * (g + 1))
        values = update_values(rate, w[0, :, cols], m[0, :, cols], v[0, :, cols], grads[g][0])
        for ref, value in zip(new, values):
            ref[0, :, cols] = value


def update_down(rate, where, w, m, v, *refs):
    one, two, new = refs[:GROUPS], refs[GROUPS : 2 * GROUPS], refs[-3:]
    FG = w.shape[0] // GROUPS
    first = pl.program_id(0) == 0
    for g in range(GROUPS):
        grad = jnp.where(first, one[g][...], two[g][...]).astype(F32)
        for j in range(2):
            at = (slice(FG * g, FG * (g + 1)), slice(CHUNK * j, CHUNK * (j + 1)))
            values = update_values(rate, w[at], m[at], v[at], grad[:, FG * j : FG * (j + 1)].T)
            for ref, value in zip(new, values):
                ref[at] = value


def pick(where, one, two, far_one, far_two):
    c, y = where[0] == 1, where[1] == 1
    near = jnp.where(c, two, one), jnp.where(c, one, two)
    far = jnp.where(c, far_two, far_one), jnp.where(c, far_one, far_two)
    return (
        jnp.where(y, far[0], near[0]), jnp.where(y, far[1], near[1]),
        jnp.where(y, near[0], far[0]), jnp.where(y, near[1], far[1]),
    )


def update_in(rate, where, w, m, v, *refs):
    grads, new = refs[:4], refs[-3:]
    Q = w.shape[1] // 24
    for j in range(6):
        four = pick(where, *(g[:, Q * j : Q * (j + 1)] for g in grads))
        for k in range(4):
            cols = slice((4 * j + k) * Q, (4 * j + k + 1) * Q)
            values = update_values(rate, w[:, cols], m[:, cols], v[:, cols], four[k])
            for ref, value in zip(new, values):
                ref[:, cols] = value


def update_out(rate, where, w, m, v, *refs):
    grads, new = refs[:4], refs[-3:]
    D = w.shape[1]
    Q = w.shape[0] // 4
    FG = grads[0].shape[1] // 2
    for r in range(4):
        for j in range(2):
            cols = slice(D // 2 * j + CHUNK * r, D // 2 * j + CHUNK * (r + 1))
            part = (slice(CHUNK * (r // 2), CHUNK * (r // 2 + 1)), slice(FG * (r % 2) + Q * j, FG * (r % 2) + Q * (j + 1)))
            four = pick(where, *(g[part] for g in grads))
            for k in range(4):
                at = (slice(Q * k, Q * (k + 1)), cols)
                values = update_values(rate, w[at], m[at], v[at], four[k].astype(F32).T)
                for ref, value in zip(new, values):
                    ref[at] = value


def update(kernel, rate, where, state, grads, before, grid, spec, g_specs, name):
    weight = state[0]
    n = grid[0] * grid[1] * spec.block_shape[-1] * spec.block_shape[-2]
    keep = [] if before is None else [pl.BlockSpec(memory_space=pl.ANY)] * 3
    first = 4 + len(grads)
    return pl.pallas_call(
        functools.partial(kernel, rate),
        grid_spec=pltpu.PrefetchScalarGridSpec(
            num_scalar_prefetch=1,
            grid=grid,
            in_specs=[spec] * 3 + list(g_specs) + keep,
            out_specs=(spec,) * 3,
        ),
        out_shape=(jax.ShapeDtypeStruct(weight.shape, F32),) * 3,
        input_output_aliases={} if before is None else {first + i: i for i in range(3)},
        compiler_params=pltpu.CompilerParams(vmem_limit_bytes=56 * 2**20),
        cost_estimate=pl.CostEstimate(flops=12 * n, bytes_accessed=20 * n, transcendentals=2 * n),
        name=name,
    )(where, *state, *grads, *(before or ()))


def fused_body(
    tokens, cotangent, in_proj, in_moment, in_square, out_proj, out_moment, out_square,
    gate_up, gate_moment, gate_square, down_proj, down_moment, down_square,
    conv_kernel, conv_moment, conv_square, norm_gains, gains_moment, gains_square,
):
    T, D = tokens.shape[1:]
    H, Q = D // 2, D // 8
    F = gate_up.shape[2] // 4
    FF, FG = 4 * F, F // GROUPS
    W2 = 2 * FG
    rate = 2.0 * D ** (-0.5)
    down_rate = 2.0 * FF ** (-0.5)
    small = jnp.concatenate(
        [conv_kernel.astype(F32), norm_gains.astype(F32), jnp.zeros((3, H), F32)], axis=0
    )
    block_out, token_grad, grads, mine, other, small_grads = run_block(
        tokens[0], cotangent[0], in_proj, out_proj, gate_up, down_proj, small
    )
    seq = lax.axis_index("seq")
    y, c = seq // 2, seq % 2
    near = jnp.stack([c, y]).astype(jnp.int32)
    far = jnp.stack([c, 1 - y]).astype(jnp.int32)

    gate_state = (gate_up, gate_moment, gate_square)
    down_state = (down_proj, down_moment, down_square)
    in_state = (in_proj, in_moment, in_square)
    out_state = (out_proj, out_moment, out_square)

    def down_step(where, one, two, before, name):
        spec = pl.BlockSpec((F, 2 * CHUNK), lambda k, q, w: (2 * w[1] + w[0] + k * (1 - 2 * w[0]), q))
        g_specs = [pl.BlockSpec((CHUNK, W2), lambda k, q, w, g=g: (2 * g + q * (1 - k) + k, 0)) for g in range(GROUPS)]
        g_specs += [pl.BlockSpec((CHUNK, W2), lambda k, q, w, g=g: (2 * g + q * k, 0)) for g in range(GROUPS)]
        return update(
            update_down, down_rate, where, down_state, (one,) * GROUPS + (two,) * GROUPS, before, (2, 2), spec, g_specs, name
        )

    across = lax.ppermute(mine, "seq", [(i, (i + 2) % 4) for i in range(4)])
    n = H // 256
    gate = update(
        update_gate, rate, near, gate_state, (grads,) * GROUPS, None,
        (2 * n, 4),
        pl.BlockSpec((1, 256, F), lambda r, k, w: (r // n, r % n, k)),
        [pl.BlockSpec((1, 256, FG), lambda r, k, w, g=g: (k, g * n + r % n, r // n)) for g in range(GROUPS)],
        "update_gate",
    )
    down = down_step(near, mine, other, None, "update_down")
    across, gate, down = lax.optimization_barrier((across, gate, down))
    beyond = lax.ppermute(across, "seq", [(i, i + 1 - 2 * (i % 2)) for i in range(4)])
    four = (mine, other, across, beyond)
    down = down_step(far, across, beyond, down, "update_down_far")
    n = 64
    base = GROUPS * H // 2
    inner = update(
        update_in, rate, near, in_state, four, None, (H // n, 1),
        pl.BlockSpec((n, 3 * D), lambda r, k, w: (r, 0)),
        [pl.BlockSpec((n, W2), lambda r, k, w: (base // n + r, 0))] * 4,
        "update_in",
    )
    base += H
    outer = update(
        update_out, rate, near, out_state, four, None, (1, 1),
        pl.BlockSpec((H, D), lambda r, k, w: (0, 0)),
        [pl.BlockSpec((2 * CHUNK, W2), lambda r, k, w: (base // (2 * CHUNK), 0))] * 4,
        "update_out",
    )
    mine_small = lax.dynamic_slice_in_dim(small_grads, lax.axis_index("shard") * H, H, axis=1)
    conv = adamw(
        conv_kernel.astype(F32), conv_moment.astype(F32), conv_square.astype(F32), mine_small[0:3], small_rate, 0.0
    )
    gains = adamw(
        norm_gains.astype(F32), gains_moment.astype(F32), gains_square.astype(F32), mine_small[3:5], small_rate, 0.0
    )
    return (block_out[None], token_grad[None], *inner, *outer, *gate, *down, *conv, *gains)


def shifted(block, axis, distance):
    devices = range(lax.axis_size(axis))
    route = [(i - distance, i) for i in devices if i - distance in devices]
    return lax.ppermute(block, axis, route)


def norm_forward(values, gain_vector):
    norm_scale = lax.rsqrt(jnp.mean(values * values, axis=-1, keepdims=True) + norm_eps)
    unit_rows = values * norm_scale
    return (unit_rows, norm_scale, (unit_rows * gain_vector).astype(jnp.bfloat16))


def norm_backward(grad_normed, unit_rows, norm_scale, gain_vector):
    gain_grad = jnp.sum(grad_normed * unit_rows, axis=(0, 1))
    grad_unit = grad_normed * gain_vector
    grad_values = norm_scale * (
        grad_unit - unit_rows * jnp.mean(grad_unit * unit_rows, axis=-1, keepdims=True)
    )
    return (gain_grad, grad_values)


def plain_body(
    tokens,
    cotangent,
    in_proj,
    in_moment,
    in_square,
    out_proj,
    out_moment,
    out_square,
    gate_up,
    gate_moment,
    gate_square,
    down_proj,
    down_moment,
    down_square,
    conv_kernel,
    conv_moment,
    conv_square,
    norm_gains,
    gains_moment,
    gains_square,
):
    gathered = (
        lax.all_gather(in_proj, "shard", axis=0, tiled=True),
        lax.all_gather(out_proj, "shard", axis=0, tiled=True),
        lax.all_gather(gate_up, "shard", axis=1, tiled=True),
        lax.all_gather(down_proj, "shard", axis=1, tiled=True),
        lax.all_gather(conv_kernel, "shard", axis=1, tiled=True),
        lax.all_gather(norm_gains, "shard", axis=1, tiled=True),
    )
    full_in, full_out, full_gate, full_down, full_conv, full_gains = gathered
    gains_float = full_gains.astype(jnp.float32)
    conv_float = full_conv.astype(jnp.float32)
    inputs = tokens.astype(jnp.float32)
    model_width = inputs.shape[2]
    rows_count = inputs.shape[1]
    unit_one, scale_one, normed_one = norm_forward(inputs, gains_float[0])
    projected = jnp.einsum("scd,de->sce", normed_one, full_in, preferred_element_type=jnp.float32)
    first_gate = projected[:, :, :model_width]
    second_gate = projected[:, :, model_width : 2 * model_width]
    conv_input = projected[:, :, 2 * model_width :]
    mixed_in = (first_gate * conv_input).astype(jnp.bfloat16)
    before = shifted(mixed_in[:, rows_count - 2 :, :], "seq", 1)
    extended = jnp.concatenate([before, mixed_in], axis=1).astype(jnp.float32)
    convolved = (
        conv_float[0] * extended[:, :-2]
        + conv_float[1] * extended[:, 1:-1]
        + conv_float[2] * extended[:, 2:]
    )
    gated_out = (second_gate * convolved).astype(jnp.bfloat16)
    middle = inputs + jnp.einsum(
        "scd,de->sce", gated_out, full_out, preferred_element_type=jnp.float32
    )
    unit_two, scale_two, normed_two = norm_forward(middle, gains_float[1])
    gate_value = jnp.einsum(
        "scd,df->scf", normed_two, full_gate[0], preferred_element_type=jnp.float32
    )
    upward = jnp.einsum("scd,df->scf", normed_two, full_gate[1], preferred_element_type=jnp.float32)
    hidden = (jax.nn.silu(gate_value) * upward).astype(jnp.bfloat16)
    result = middle + jnp.einsum(
        "scf,fd->scd", hidden, full_down, preferred_element_type=jnp.float32
    )
    block_out = result.astype(jnp.bfloat16)
    regathered = (
        lax.all_gather(in_proj, "shard", axis=0, tiled=True),
        lax.all_gather(out_proj, "shard", axis=0, tiled=True),
        lax.all_gather(gate_up, "shard", axis=1, tiled=True),
        lax.all_gather(down_proj, "shard", axis=1, tiled=True),
        lax.all_gather(conv_kernel, "shard", axis=1, tiled=True),
        lax.all_gather(norm_gains, "shard", axis=1, tiled=True),
    )
    full_in, full_out, full_gate, full_down, full_conv, full_gains = regathered
    gains_float = full_gains.astype(jnp.float32)
    conv_float = full_conv.astype(jnp.float32)
    grad_result = cotangent.astype(jnp.float32)
    grad_hidden = jnp.einsum(
        "scd,fd->scf", cotangent, full_down, preferred_element_type=jnp.float32
    )
    grad_down = jnp.einsum("scf,scd->fd", hidden, cotangent, preferred_element_type=jnp.float32)
    sigmoid_gate = jax.nn.sigmoid(gate_value)
    grad_gate = (
        grad_hidden * upward * sigmoid_gate * (1.0 + gate_value * (1.0 - sigmoid_gate))
    ).astype(jnp.bfloat16)
    grad_upward = (grad_hidden * jax.nn.silu(gate_value)).astype(jnp.bfloat16)
    grad_gate_up = jnp.stack(
        [
            jnp.einsum("scd,scf->df", normed_two, grad_gate, preferred_element_type=jnp.float32),
            jnp.einsum("scd,scf->df", normed_two, grad_upward, preferred_element_type=jnp.float32),
        ]
    )
    grad_normed_two = jnp.einsum(
        "scf,df->scd", grad_gate, full_gate[0], preferred_element_type=jnp.float32
    ) + jnp.einsum("scf,df->scd", grad_upward, full_gate[1], preferred_element_type=jnp.float32)
    gain_two, grad_from_two = norm_backward(grad_normed_two, unit_two, scale_two, gains_float[1])
    grad_middle = grad_result + grad_from_two
    middle_low = grad_middle.astype(jnp.bfloat16)
    grad_out = jnp.einsum("scd,sce->de", gated_out, middle_low, preferred_element_type=jnp.float32)
    grad_gated = jnp.einsum("sce,de->scd", middle_low, full_out, preferred_element_type=jnp.float32)
    grad_second = grad_gated * convolved
    grad_conv_out = grad_gated * second_gate
    grad_conv = jnp.stack(
        [
            jnp.sum(grad_conv_out * extended[:, offset : offset + rows_count], axis=(0, 1))
            for offset in range(3)
        ]
    )
    grad_extended = (
        jnp.pad(grad_conv_out * conv_float[0], ((0, 0), (0, 2), (0, 0)))
        + jnp.pad(grad_conv_out * conv_float[1], ((0, 0), (1, 1), (0, 0)))
        + jnp.pad(grad_conv_out * conv_float[2], ((0, 0), (2, 0), (0, 0)))
    )
    from_next = shifted(grad_extended[:, :2, :], "seq", -1)
    grad_mixed = grad_extended[:, 2:, :] + jnp.pad(from_next, ((0, 0), (rows_count - 2, 0), (0, 0)))
    grad_projected = jnp.concatenate(
        [grad_mixed * conv_input, grad_second, grad_mixed * first_gate], axis=2
    ).astype(jnp.bfloat16)
    grad_in = jnp.einsum(
        "scd,sce->de", normed_one, grad_projected, preferred_element_type=jnp.float32
    )
    grad_normed_one = jnp.einsum(
        "sce,de->scd", grad_projected, full_in, preferred_element_type=jnp.float32
    )
    gain_one, grad_from_one = norm_backward(grad_normed_one, unit_one, scale_one, gains_float[0])
    token_grad = (grad_middle + grad_from_one).astype(jnp.bfloat16)
    grad_gains = jnp.stack([gain_one, gain_two])
    parts = (
        lax.psum_scatter(grad_in, "shard", scatter_dimension=0, tiled=True),
        lax.psum_scatter(grad_out, "shard", scatter_dimension=0, tiled=True),
        lax.psum_scatter(grad_gate_up, "shard", scatter_dimension=1, tiled=True),
        lax.psum_scatter(grad_down, "shard", scatter_dimension=1, tiled=True),
        lax.psum_scatter(grad_conv, "shard", scatter_dimension=1, tiled=True),
        lax.psum_scatter(grad_gains, "shard", scatter_dimension=1, tiled=True),
    )
    totals = lax.psum((parts[0], parts[1], parts[2], parts[3], parts[4], parts[5]), ("rep", "seq"))
    matrix_rate = 2.0 * model_width ** (-0.5)
    down_rate = 2.0 * gate_up.shape[2] ** (-0.5)
    in_next, in_moment_next, in_square_next = adamw(
        in_proj.astype(jnp.float32),
        in_moment.astype(jnp.float32),
        in_square.astype(jnp.float32),
        totals[0],
        matrix_rate,
        decay_rate,
    )
    out_next, out_moment_next, out_square_next = adamw(
        out_proj.astype(jnp.float32),
        out_moment.astype(jnp.float32),
        out_square.astype(jnp.float32),
        totals[1],
        matrix_rate,
        decay_rate,
    )
    gate_next, gate_moment_next, gate_square_next = adamw(
        gate_up.astype(jnp.float32),
        gate_moment.astype(jnp.float32),
        gate_square.astype(jnp.float32),
        totals[2],
        matrix_rate,
        decay_rate,
    )
    down_next, down_moment_next, down_square_next = adamw(
        down_proj.astype(jnp.float32),
        down_moment.astype(jnp.float32),
        down_square.astype(jnp.float32),
        totals[3],
        down_rate,
        decay_rate,
    )
    conv_next, conv_moment_next, conv_square_next = adamw(
        conv_kernel.astype(jnp.float32),
        conv_moment.astype(jnp.float32),
        conv_square.astype(jnp.float32),
        totals[4],
        small_rate,
        0.0,
    )
    gains_next, gains_moment_next, gains_square_next = adamw(
        norm_gains.astype(jnp.float32),
        gains_moment.astype(jnp.float32),
        gains_square.astype(jnp.float32),
        totals[5],
        small_rate,
        0.0,
    )
    return (
        block_out,
        token_grad,
        in_next,
        in_moment_next,
        in_square_next,
        out_next,
        out_moment_next,
        out_square_next,
        gate_next,
        gate_moment_next,
        gate_square_next,
        down_next,
        down_moment_next,
        down_square_next,
        conv_next,
        conv_moment_next,
        conv_square_next,
        gains_next,
        gains_moment_next,
        gains_square_next,
    )


def solution(mesh):
    act = P(("rep", "shard"), "seq", None)
    weights = (
        (P("shard", None),) * 6 + (P(None, "shard", None),) * 3 + (P(None, "shard"),) * 9
    )
    specs = (act, act) + weights
    sizes = (mesh.shape["rep"], mesh.shape["seq"], mesh.shape["shard"])
    body = fused_body if sizes == (4, 4, 2) else plain_body
    return jax.shard_map(body, mesh=mesh, in_specs=specs, out_specs=specs, check_vma=False)
```

```python
import functools

import jax
import jax.numpy as jnp
from jax import lax
from jax.experimental import pallas as pl
from jax.experimental.pallas import tpu as pltpu
from jax.sharding import PartitionSpec as P

STEP = 10
norm_eps = 1e-05
beta_one = 0.9
beta_two = 0.95
adam_eps = 1e-08
decay_rate = 0.1
small_rate = 0.4

BF = jnp.bfloat16
F32 = jnp.float32
MESH = pl.DeviceIdType.MESH
GROUPS = 3
CHUNK = 128
TILE = 16
PLAN = (
    (0, 0, 0, 0, 1),
    (0, 0, 0, 0, 2),
    (0, 0, 0, 1, 3),
    (0, 0, 1, 3, 5),
    (0, 0, 2, 4, 6),
    (0, 1, 3, 5, 8),
    (0, 2, 4, 6, 10),
    (0, 4, 6, 8, 11),
    (0, 12, 15, 17, 21),
    (6, 15, 17, 20, 24),
    (9, 17, 20, 22, 26),
    (15, 21, 24, 26, 29),
    (19, 25, 28, 30, 33),
)
HELD = 40

SLOTS = 64
SPOTS = 16


def dot(a, b):
    return lax.dot_general(a, b, (((1,), (0,)), ((), ())), preferred_element_type=F32)


def dot_nt(a, b):
    return lax.dot_general(a, b, (((1,), (1,)), ((), ())), preferred_element_type=F32)


def dot_tn(a, b):
    return lax.dot_general(a, b, (((0,), (0,)), ((), ())), preferred_element_type=F32)


def block_kernel(
    dims,
    tok_h, cot_h, in_h, out_h, gu_h, dn_h, small_h,
    block_out, token_grad, grads, mine, other, small_grads,
    WG, WD, WIN, WOUT, SM, TOK, N1, N2, CT, ML,
    PROJ, MX, CONV, GATED, GCO, ACT, HID, FA, FB, GS, GO, RX,
    MID, GM, P32, SC, RC, SY, RY, SG,
    ss, rs, ls, xs, xr, z1s, z1r, z2s, z2r, ts, tr, ys, yr, c1s, c1r, c2s, c2r, gl,
    ready_w, ready_a,
):
    D, T, FQ, F = dims
    H, Q, R, FG = D // 2, FQ // 2, 4 * T, F // GROUPS
    MT = H // 2
    GR = H + H // 2
    NCH = 2 * (GROUPS + 1) * GR // CHUNK
    PER = 2 * GR // CHUNK
    NGU = 2 * H // CHUNK
    z = lax.axis_index("rep")
    s = lax.axis_index("seq")
    x = lax.axis_index("shard")
    y, c = s // 2, s % 2
    h = z % 2
    is_mid = jnp.logical_and(z > 0, z < 3)
    is_end = jnp.logical_or(z == 0, z == 3)
    xo = 1 - x
    xp = (z, s, xo)
    cp = (z, 2 * y + 1 - c, x)
    yp = (z, 2 * (1 - y) + c, x)
    zp = (z + 1 - 2 * h, s, x)
    mp = (3 - z, s, x)

    def block(i):
        return 2 * (y + (i // 2) * (1 - 2 * y)) + c + (i % 2) * (1 - 2 * c)

    def at(start, size, unit):
        return pl.ds(pl.multiple_of(start, unit), size)

    def rows(m, n=T):
        return at(m * n, n, n)

    slots, spots = {}, {}

    def remote(name, src, dst, dev):
        k = slots.setdefault(name, len(slots))
        return pltpu.make_async_remote_copy(
            src_ref=src, dst_ref=dst, send_sem=ss.at[k], recv_sem=rs.at[k], device_id=dev, device_id_type=MESH
        )

    def local(name, src, dst):
        return pltpu.make_async_copy(src, dst, ls.at[spots.setdefault(name, len(spots))])

    barrier = pltpu.get_barrier_semaphore()
    for dev in (xp, cp, yp, zp):
        pl.semaphore_signal(barrier, inc=1, device_id=dev, device_id_type=MESH)

    @pl.when(is_mid)
    def _():
        pl.semaphore_signal(barrier, inc=1, device_id=mp, device_id_type=MESH)

    def weight(name, owner, half=None):
        kind, p = name.split("_")
        p = int(p)
        if half is None:
            half, parts = 0, 1
        else:
            parts = 2
        n = H // parts
        if kind == "in":
            return WIN.at[at(H * owner + n * half, n, n), FQ * p : FQ * (p + 1)]
        if kind == "out":
            n = Q // parts
            return WOUT.at[at(Q * owner + n * half, n, n)]
        if kind == "down":
            n = FG // parts
            return WD.at[at(FG * p + n * half, n, n), at(H * owner, H, H)]
        j = 0 if kind == "gate" else 1
        return WG.at[at(GR + D * p + H * owner + n * half, n, H // 2), FG * j : FG * (j + 1)]

    def weight_source(name, half=None):
        kind, p = name.split("_")
        p = int(p)
        parts = 1 if half is None else 2
        first = 0 if half is None else half
        n = H // parts
        if kind == "in":
            dst = at(H * x + n * first, n, n)
            return [
                (in_h.at[at(n * first, n, n), at(D * p + H * k + Q * s, Q, Q)], WIN.at[dst, pl.ds(FQ * p + Q * k, Q)])
                for k in range(2)
            ]
        dst = weight(name, x, half)
        if kind == "out":
            n = Q // parts
            return [(out_h.at[at(Q * s + n * first, n, n)], dst)]
        if kind == "down":
            n = FG // parts
            return [(dn_h.at[at(F * s + FG * p + n * first, n, n)], dst)]
        j = 0 if kind == "gate" else 1
        return [(gu_h.at[j, at(n * first, n, n), at(F * s + FG * p, FG, FG)], dst)]

    loads = [
        local("tok", tok_h, TOK),
        local("small", small_h, SM.at[x]),
        local("ct", cot_h, CT.at[rows(s)]),
    ]
    order = ["in_0", "in_1", "in_2", "out_0"]
    for g in range(GROUPS):
        order += ["gate_%d" % g, "up_%d" % g, "down_%d" % g]
    for name in order:
        for src, dst in weight_source(name):
            loads.append(local("in" if name[:3] == "in_" else name.replace("out_0", "out"), src, dst))
    for copy in loads:
        copy.start()

    def local_wait(name):
        if name == "tok":
            copy = local(name, tok_h, TOK)
        elif name == "small":
            copy = local(name, small_h, SM.at[x])
        elif name == "ct":
            copy = local(name, cot_h, CT.at[rows(s)])
        elif name == "in":
            copy = local(name, WIN.at[rows(x, H)], WIN.at[rows(x, H)])
        else:
            here = weight(name if name != "out" else "out_0", x)
            copy = local(name, here, here)
        copy.wait()

    @pl.when(is_mid)
    def _():
        pl.semaphore_wait(barrier, 5)

    @pl.when(is_end)
    def _():
        pl.semaphore_wait(barrier, 4)

    def weight_pass(name):
        here = weight(name, xo, h)
        remote(name, here, here, xp).wait_recv()
        remote(name + "_z", here, here, zp).start()

    def weight_wait(name):
        there = weight(name, xo, 1 - h)
        remote(name + "_z", there, there, zp).wait_recv()

    def weight_passed(name):
        here = weight(name, xo, h)
        remote(name + "_z", here, here, zp).wait_send()

    def group_wait(g):
        for kind in ("gate_", "up_", "down_"):
            local_wait(kind + str(g))
            weight_wait(kind + str(g))

    def gather_copy(name, buf, kind, src=None):
        m = block(2) if kind == "f" else s
        return remote(
            name + "_" + kind, buf.at[rows(m)] if src is None else src, buf.at[rows(m)], yp if kind == "y" else cp
        )

    def gather_start(name, buf):
        gather_copy(name, buf, "y").start()
        gather_copy(name, buf, "c").start()

    def gather_step(name, buf, i, between=None):
        @pl.when(i == 1)
        def _():
            remote(name + "_c", buf.at[rows(block(1))], buf.at[rows(block(1))], cp).wait_recv()

        @pl.when(i == 2)
        def _():
            remote(name + "_y", buf.at[rows(block(2))], buf.at[rows(block(2))], yp).wait_recv()
            if between is not None:
                between()
            gather_copy(name, buf, "f").start()

        @pl.when(i == 3)
        def _():
            remote(name + "_f", buf.at[rows(block(3))], buf.at[rows(block(3))], cp).wait_recv()

    remote("small", small_h, SM.at[x], xp).start()
    gather_copy("n1", N1, "y", tok_h).start()
    gather_copy("ct", CT, "y", cot_h).start()
    gather_copy("ct", CT, "c", cot_h).start()
    for name in order:
        for src, dst in weight_source(name, h):
            remote(name, src, dst, xp).start()

    def sum_core(name, lot, k):
        return remote(name + "_" + str(k), SC.at[lot, k], RC.at[lot, k], cp)

    def sum_y(name, lot):
        return remote(name + "_y", SY.at[lot], RY.at[lot], yp)

    def sum_emit(name, lot, i, partial):
        @pl.when(i % 2 == 0)
        def _():
            P32[i // 2] = partial

        @pl.when(i == 1)
        def _():
            SC[lot, 1] = partial.astype(BF)
            sum_core(name, lot, 1).start()

        @pl.when(i == 3)
        def _():
            SC[lot, 0] = partial.astype(BF)
            sum_core(name, lot, 0).start()

    def sum_cross(name, lot):
        sum_core(name, lot, 0).wait_recv()

        def add(r):
            SY[lot, r] = (P32[1, r] + RC[lot, 0, r].astype(F32)).astype(BF)

        tiles(T, add, 32)
        sum_y(name, lot).start()

    def sum_wait(name, lot):
        sum_core(name, lot, 1).wait_recv()
        sum_y(name, lot).wait_recv()

    def sum_rows(lot, r):
        return P32[0, r] + RC[lot, 1, r].astype(F32) + RY[lot, r].astype(F32)

    def sum_done(name, lot):
        sum_core(name, lot, 0).wait_send()
        sum_core(name, lot, 1).wait_send()
        sum_y(name, lot).wait_send()

    def tiles(n, body, size=TILE):
        def step(t, carry):
            body(pl.ds(pl.multiple_of(t * size, size), size))
            return carry

        lax.fori_loop(0, n // size, step, 0)

    def blocks(body, order=(0, 1, 2, 3)):
        first, step = order[0], order[1] - order[0]

        def turn(t, carry):
            i = first + step * t
            body(i, block(i))
            return carry

        lax.fori_loop(0, len(order), turn, 0)

    def gain(k):
        return jnp.concatenate([SM[0, 3 + k : 4 + k, :], SM[1, 3 + k : 4 + k, :]], axis=1)

    def tap(k):
        cols = rows(s, Q)
        return jnp.concatenate([SM[0, k : k + 1, cols], SM[1, k : k + 1, cols]], axis=1)

    local_wait("tok")
    local_wait("small")
    remote("small", small_h, SM.at[xo], xp).wait()
    SG[0] = jnp.zeros_like(SG[0])
    MX[0:8] = jnp.zeros((8, FQ), F32)
    GCO[R : R + 8] = jnp.zeros((8, FQ), F32)
    gain_one = gain(0)

    def norm_one(src, first, m):
        def one(r):
            v = src[at(first + r.start, 32, 32)].astype(F32)
            scale = lax.rsqrt(jnp.mean(v * v, axis=-1, keepdims=True) + norm_eps)
            N1[at(m * T + r.start, 32, 32)] = (v * scale * gain_one).astype(BF)

        tiles(T, one, 32)

    norm_one(TOK, 0, s)
    gather_copy("n1", N1, "c").start()

    for name in order[:3]:
        weight_pass(name)
    local_wait("in")
    for name in order[:3]:
        weight_wait(name)
    weight_pass("out_0")

    def project(i, m):
        gather_step("n1", N1, i, lambda: norm_one(N1, block(2) * T, block(2)))
        p = dot(N1[rows(m)], WIN[...])
        PROJ[rows(m)] = p
        mixed = (p[:, :FQ] * p[:, 2 * FQ :]).astype(BF)
        MX[at(8 + m * T, T, 8)] = mixed.astype(F32)

    blocks(project)
    weight_pass("gate_0")
    local_wait("out")
    weight_wait("out_0")

    def convolve(i, m):
        ext = MX[at(m * T, T + 8, 8)]
        conv = tap(0) * ext[6 : 6 + T] + tap(1) * ext[7 : 7 + T] + tap(2) * ext[8 : 8 + T]
        CONV[rows(m)] = conv
        gated = (PROJ[rows(m), FQ : 2 * FQ] * conv).astype(BF)
        GATED[rows(m)] = gated
        sum_emit("ro", 0, i, dot(gated, WOUT[...]))

    blocks(convolve, (3, 2))
    weight_pass("up_0")
    sum_cross("ro", 0)
    blocks(convolve, (1, 0))
    for name in ("down_0", "gate_1", "up_1"):
        weight_pass(name)
    sum_wait("ro", 0)

    gain_two = gain(1)

    def norm_two(r):
        v = TOK[r].astype(F32) + sum_rows(0, r)
        MID[r] = v
        scale = lax.rsqrt(jnp.mean(v * v, axis=-1, keepdims=True) + norm_eps)
        N2[at(s * T + r.start, 32, 32)] = (v * scale * gain_two).astype(BF)

    tiles(T, norm_two, 32)
    gather_start("n2", N2)
    sum_done("ro", 0)
    weight_pass("down_1")

    def feed(g):
        def unit(i, m):
            if g == 0:
                gather_step("n2", N2, i)
                gather_step("ct", CT, i)
            FA[...] = dot(N2[rows(m)], WG[GR + D * g : GR + D * (g + 1)])
            FB[...] = dot_nt(CT[rows(m)], WD[FG * g : FG * (g + 1)])

            def act(r):
                gate, up, gh = FA[r, 0:FG], FA[r, FG:], FB[r]
                sig = jax.nn.sigmoid(gate)
                silu = gate * sig
                ro = at(GR + R * g + m * T + r.start, 32, 32)
                ACT[ro, 0:FG] = (gh * up * sig * (1.0 + gate * (1.0 - sig))).astype(BF)
                ACT[ro, FG:] = (gh * silu).astype(BF)
                HID[at(m * T + r.start, 32, 32), FG * g : FG * (g + 1)] = (silu * up).astype(BF)

            tiles(T, act, 32)

        return unit

    def group_grad(g, dst, owner):
        base = GR * g

        def step(t, carry):
            lhs = N2[:, at(H * owner + MT * t, MT, MT)]
            dst[at(base + MT * t, MT, MT)] = dot_tn(lhs, ACT[GR + R * g : GR + R * (g + 1)]).astype(BF)
            lhs = CT[:, at(H * owner + MT * t, MT, MT)]
            low = dot_tn(lhs, HID[:, FG * g : FG * (g + 1)]).astype(BF)
            for j in range(2):
                dst[at(base + H + CHUNK * t, CHUNK, CHUNK), FG * j : FG * (j + 1)] = low[CHUNK * j : CHUNK * (j + 1)]
            return carry

        lax.fori_loop(0, H // MT, step, 0)

    def chunk(ref, k):
        return ref.at[rows(k // 2, CHUNK), at(FG * (k % 2), FG, FG)]

    def step_copy(src, dst, send, recv, k, dev):
        return pltpu.make_async_remote_copy(
            src_ref=src, dst_ref=dst, send_sem=send.at[k], recv_sem=recv.at[k], device_id=dev, device_id_type=MESH
        )

    def x_copy(k):
        return step_copy(chunk(GS, k), chunk(RX, k), xs, xr, k, xp)

    def z1_copy(k):
        return step_copy(chunk(GO, k), chunk(WG, k), z1s, z1r, k, zp)

    def z2_copy(k):
        return step_copy(chunk(RX, k), chunk(ACT, k), z2s, z2r, k, mp)

    def t_copy(k):
        return step_copy(chunk(GO, k), chunk(WG, k), ts, tr, k, zp)

    def is_wide(k):
        return jnp.logical_and(k < GROUPS * PER, k % PER < NGU)

    def wide_at(k, m):
        return grads.at[m, rows((NGU // 2) * (k // PER) + (k % PER) // 2, CHUNK), at(FG * (k % 2), FG, FG)]

    def late_at(k, ref, inner):
        if inner:
            row = ((PER - NGU) // 2) * GROUPS + (k - GROUPS * PER) // 2
        else:
            row = ((PER - NGU) // 2) * (k // PER) + (k % PER - NGU) // 2
        return ref.at[rows(row, CHUNK), at(FG * (k % 2), FG, FG)]

    def y_copy(k, src):
        return step_copy(chunk(src, k), wide_at(k, s), ys, yr, k, yp)

    def c2_copy(k):
        m = block(2)
        return step_copy(wide_at(k, m), wide_at(k, m), c2s, c2r, k, cp)

    def spread(k, src):
        @pl.when(is_wide(k))
        def _():
            y_copy(k, src).start()
            step_copy(chunk(src, k), wide_at(k, s), c1s, c1r, k, cp).start()
            pltpu.make_async_copy(chunk(src, k), wide_at(k, s), gl.at[k]).start()

        for inner in (False, True):
            if inner:
                cond = k >= GROUPS * PER
            else:
                cond = jnp.logical_and(k < GROUPS * PER, k % PER >= NGU)

            @pl.when(cond)
            def _():
                step_copy(chunk(src, k), late_at(k, other, inner), c1s, c1r, k, cp).start()
                pltpu.make_async_copy(chunk(src, k), late_at(k, mine, inner), gl.at[k]).start()

    def add(k, dst, one, two):
        total = chunk(one, k)[...].astype(F32) + chunk(two, k)[...].astype(F32)
        chunk(dst, k)[...] = total.astype(BF)

    def add_x(k):
        x_copy(k).wait_recv()
        add(k, GO, GO, RX)
        pl.when(is_end)(lambda: z1_copy(k).start())

    def add_end(k):
        @pl.when(is_mid)
        def _():
            z1_copy(k).wait_recv()
            add(k, RX, GO, WG)
            z2_copy(k).start()

    def add_mid(k):
        @pl.when(is_mid)
        def _():
            z2_copy(k).wait_recv()
            add(k, GO, RX, ACT)
            t_copy(k).start()
            spread(k, GO)

    def take(k):
        @pl.when(is_end)
        def _():
            t_copy(k).wait_recv()
            spread(k, WG)

    def hand(k):
        @pl.when(is_wide(k))
        def _():
            m = block(2)
            step_copy(wide_at(k, m), wide_at(k, m), ys, yr, k, yp).wait_recv()
            c2_copy(k).start()

    stages = (hand, take, add_mid, add_end, add_x)
    place = [0] * len(stages)

    def advance(*goals, late=True):
        first = tuple(place)
        n = max(goal - at for goal, at in zip(goals, first))

        def step(t, carry):
            for body, at, goal in zip(stages, first, goals):
                if goal > at:
                    skip = n - (goal - at) if late else 0
                    pl.when(jnp.logical_and(t >= skip, t < skip + goal - at))(functools.partial(body, at + t - skip))
            return carry

        lax.fori_loop(0, n, step, 0)
        place[:] = goals

    def send(first, last):
        def step(k, carry):
            x_copy(k).start()
            return carry

        lax.fori_loop(first, last, step, 0)

    local_wait("ct")
    group_wait(0)
    blocks(feed(0), (0, 1))
    weight_pass("gate_2")
    group_wait(1)
    weight_pass("up_2")
    blocks(feed(1), (0, 1))
    blocks(feed(0), (2, 3))
    group_grad(0, GS, xo)
    send(0, PER)
    weight_pass("down_2")
    group_grad(0, GO, x)
    advance(*PLAN[0])
    blocks(feed(1), (2, 3))
    advance(*PLAN[1])
    group_grad(1, GS, xo)
    send(PER, 2 * PER)
    advance(*PLAN[2])
    group_wait(2)
    blocks(feed(2), (0, 1, 2, 3))
    advance(*PLAN[3])
    group_grad(2, GS, xo)
    send(2 * PER, 3 * PER)
    advance(*PLAN[4])

    def back_feed(i, m):
        partial = dot_nt(ACT[at(GR + m * T, T, T)], WG[GR : GR + D])
        for g in range(1, GROUPS):
            partial = partial + dot_nt(ACT[at(GR + R * g + m * T, T, T)], WG[GR + D * g : GR + D * (g + 1)])
        sum_emit("rg", 1, i, partial)

    blocks(back_feed, (3, 2))
    sum_cross("rg", 1)
    advance(*PLAN[5])
    blocks(back_feed, (1, 0))
    for g in range(GROUPS):
        weight_passed("gate_%d" % g)
        weight_passed("up_%d" % g)
    pl.semaphore_signal(ready_w, inc=1, device_id=zp, device_id_type=MESH)
    group_grad(1, GO, x)
    advance(*PLAN[6])
    group_grad(2, GO, x)

    @pl.when(is_mid)
    def _():
        pl.semaphore_signal(ready_a, inc=1, device_id=mp, device_id_type=MESH)

    pl.semaphore_wait(ready_w, 1)

    @pl.when(is_mid)
    def _():
        pl.semaphore_wait(ready_a, 1)

    advance(*PLAN[7])

    sum_wait("rg", 1)

    def back_two(t, acc):
        r = at(t * TILE, TILE, TILE)
        v = MID[r]
        scale = lax.rsqrt(jnp.mean(v * v, axis=-1, keepdims=True) + norm_eps)
        unit = v * scale
        e = sum_rows(1, r)
        eu = e * unit
        ew = e * gain_two
        grad = scale * (ew - unit * jnp.mean(ew * unit, axis=-1, keepdims=True))
        ro = at(s * T + t * TILE, TILE, TILE)
        gm = CT[ro].astype(F32) + grad
        GM[r] = gm
        ML[ro] = gm.astype(BF)
        return acc + jnp.sum(eu, axis=0, keepdims=True)

    SG[0, 4:5, :] = lax.fori_loop(0, T // TILE, back_two, jnp.zeros((1, D), F32))
    gather_start("ml", ML)
    sum_done("rg", 1)
    advance(*PLAN[8])

    def gated_back(i, m):
        gather_step("ml", ML, i)
        gg = dot_nt(ML[rows(m)], WOUT[...])
        gco = gg * PROJ[rows(m), FQ : 2 * FQ]
        GCO[rows(m)] = gco
        PROJ[rows(m), FQ : 2 * FQ] = gg * CONV[rows(m)]

    blocks(gated_back)
    for kind in "cyf":
        gather_copy("n2", N2, kind).wait_send()

    def conv_back(t, acc):
        i = 3 - t
        m = block(i)
        gco = GCO[at(m * T, T + 8, 8)]
        ext = MX[at(m * T, T + 8, 8)]
        here = gco[0:T]
        gm = tap(2) * here + tap(1) * gco[1 : 1 + T] + tap(0) * gco[2 : 2 + T]
        p = PROJ[rows(m)]
        low = jnp.concatenate([gm * p[:, 2 * FQ :], p[:, FQ : 2 * FQ], gm * p[:, :FQ]], axis=1).astype(BF)
        N2[rows(m), 0 : 3 * FQ] = low
        sum_emit("ri", 1, i, dot_nt(low, WIN[...]))
        return tuple(
            a + jnp.sum(here * ext[6 + k : 6 + k + T], axis=0, keepdims=True) for k, a in enumerate(acc)
        )

    conv_grads = lax.fori_loop(0, 4, conv_back, (jnp.zeros((1, FQ), F32),) * 3)
    for k in range(3):
        SG[0, k : k + 1, rows(s, Q)] = conv_grads[k][:, :Q]
        SG[0, k : k + 1, at(H + s * Q, Q, Q)] = conv_grads[k][:, Q:]
    sum_cross("ri", 1)

    def io_grad(dst, owner):
        base = GROUPS * GR

        def step(t, carry):
            lhs = N1[:, at(H * owner + MT * t, MT, MT)]
            dst[at(base + MT * t, MT, MT)] = dot_tn(lhs, N2[:, 0 : 3 * FQ]).astype(BF)
            right = GATED[:, rows(owner, Q)]
            for j in range(2):
                lhs = ML[:, at(H * j + MT * t, MT, MT)]
                low = dot_tn(lhs, right).astype(BF)
                for k in range(2):
                    dst[at(base + H + CHUNK * t, CHUNK, CHUNK), FG * k + Q * j : FG * k + Q * (j + 1)] = low[
                        CHUNK * k : CHUNK * (k + 1)
                    ]
            for k in range(2):
                dst[at(base + H + CHUNK * t, CHUNK, CHUNK), FG * k + 2 * Q : FG * (k + 1)] = jnp.zeros(
                    (CHUNK, FG - 2 * Q), BF
                )
            return carry

        lax.fori_loop(0, H // MT, step, 0)

    io_grad(GS, xo)
    send(GROUPS * PER, HELD)
    advance(*PLAN[9])
    io_grad(GO, x)
    advance(*PLAN[10])

    sum_wait("ri", 1)
    low_out = SC.at[0, 0]

    def back_one(t, acc):
        r = at(t * TILE, TILE, TILE)
        v = TOK[r].astype(F32)
        scale = lax.rsqrt(jnp.mean(v * v, axis=-1, keepdims=True) + norm_eps)
        unit = v * scale
        e = sum_rows(1, r)
        eu = e * unit
        ew = e * gain_one
        grad = scale * (ew - unit * jnp.mean(ew * unit, axis=-1, keepdims=True))
        low_out[r] = (GM[r] + grad).astype(BF)
        return acc + jnp.sum(eu, axis=0, keepdims=True)

    SG[0, 3:4, :] = lax.fori_loop(0, T // TILE, back_one, jnp.zeros((1, D), F32))
    out_copy = pltpu.make_async_copy(low_out, token_grad, ls.at[spots["tok"]])
    out_copy.start()
    sum_done("ri", 1)

    def small_start(name, dev, k):
        remote(name, SG.at[0], SG.at[k], dev).start()

    def small_end(name, dev, k):
        remote(name, SG.at[0], SG.at[k], dev).wait()
        SG[0] = SG[0] + SG[k]

    small_start("sg_c", cp, 2)
    advance(*PLAN[11])
    small_end("sg_c", cp, 2)
    small_start("sg_y", yp, 3)
    out_copy.wait()

    def down(i, m):
        sum_emit("rr", 0, i, dot(HID[rows(m)], WD[...]))

    blocks(down, (3, 2, 1, 0))
    sum_cross("rr", 0)
    small_end("sg_y", yp, 3)
    small_start("sg_x", xp, 1)
    send(HELD, NCH)
    advance(*PLAN[12])

    def on(first, last):
        for k in range(first, last + 1, 2):
            advance(*(min(max(k - lag, at), NCH) for lag, at in zip((12, 9, 6, 3, 0), place)))

    on(32, 38)
    sum_wait("rr", 0)
    sum_done("rr", 0)

    def result(r):
        low_out[r] = (MID[r] + sum_rows(0, r)).astype(BF)

    tiles(T, result, 32)
    out_copy = pltpu.make_async_copy(low_out, block_out, ls.at[spots["tok"]])
    out_copy.start()
    on(40, 42)
    small_end("sg_x", xp, 1)
    pl.when(is_end)(lambda: small_start("sg_a", zp, 4))
    on(44, 46)

    @pl.when(is_end)
    def _():
        remote("sg_a", SG.at[0], SG.at[4], zp).wait_send()

    @pl.when(is_mid)
    def _():
        remote("sg_a", SG.at[0], SG.at[4], zp).wait_recv()
        SG[0] = SG[0] + SG[4]
        small_start("sg_b", mp, 5)

    on(48, 48)

    @pl.when(is_mid)
    def _():
        remote("sg_b", SG.at[0], SG.at[5], mp).wait()
        SG[6] = SG[0] + SG[5]
        remote("sg_t", SG.at[6], SG.at[6], zp).start()

    advance(*(NCH,) * 5, late=False)

    @pl.when(is_mid)
    def _():
        remote("sg_t", SG.at[6], SG.at[6], zp).wait_send()

    @pl.when(is_end)
    def _():
        remote("sg_t", SG.at[6], SG.at[6], zp).wait_recv()

    small_copy = pltpu.make_async_copy(SG.at[6], small_grads, ls.at[spots["small"]])
    small_copy.start()

    def finish(k, carry):
        x_copy(k).wait_send()

        @pl.when(is_end)
        def _():
            z1_copy(k).wait_send()

        @pl.when(is_mid)
        def _():
            z2_copy(k).wait_send()
            t_copy(k).wait_send()

        @pl.when(is_wide(k))
        def _():
            y_copy(k, GO).wait_send()
            c2_copy(k).wait()

        here = chunk(GO, k)
        step_copy(here, here, c1s, c1r, k, cp).wait()
        pltpu.make_async_copy(here, here, gl.at[k]).wait()
        return carry

    lax.fori_loop(0, NCH, finish, 0)
    out_copy.wait()
    small_copy.wait()
    for name in order:
        here = weight(name, x, h)
        remote(name, here, here, xp).wait_send()
        if name[0] not in "gu":
            weight_passed(name)
    for name, buf in (("n1", N1), ("ct", CT), ("ml", ML)):
        for kind in "cyf":
            gather_copy(name, buf, kind).wait_send()


def run_block(tokens, cotangent, in_proj, out_proj, gate_up, down_proj, small):
    T, D = tokens.shape
    F = gate_up.shape[2] // 4
    FQ = D // 4
    R = 4 * T
    H = D // 2
    W2 = 2 * F // GROUPS
    GR = H + H // 2
    NR = (GROUPS + 1) * GR
    dims = (D, T, FQ, F)
    NCH = 2 * NR // CHUNK
    hbm = pl.BlockSpec(memory_space=pltpu.HBM)
    dma = pltpu.SemaphoreType.DMA
    vmem = pltpu.VMEM
    late = jax.ShapeDtypeStruct((GROUPS * H // 2 + GR, W2), BF)
    scratch = [
        vmem((GR + NR, W2), BF),
        vmem((F, D), BF),
        vmem((D, 3 * FQ), BF),
        vmem((FQ, D), BF),
        vmem((2, 8, H), F32),
        vmem((T, D), BF),
        vmem((R, D), BF),
        vmem((R, D), BF),
        vmem((R, D), BF),
        vmem((R, D), BF),
        vmem((R, 3 * FQ), F32),
        vmem((R + 8, FQ), F32),
        vmem((R, FQ), F32),
        vmem((R, FQ), BF),
        vmem((R + 8, FQ), F32),
        vmem((GR + NR, W2), BF),
        vmem((R, F), BF),
        vmem((T, W2), F32),
        vmem((T, W2 // 2), F32),
        vmem((NR, W2), BF),
        vmem((NR, W2), BF),
        vmem((NR, W2), BF),
        vmem((T, D), F32),
        vmem((T, D), F32),
        vmem((2, T, D), F32),
        vmem((2, 2, T, D), BF),
        vmem((2, 2, T, D), BF),
        vmem((2, T, D), BF),
        vmem((2, T, D), BF),
        vmem((7, 8, D), F32),
        dma((SLOTS,)),
        dma((SLOTS,)),
        dma((SPOTS,)),
    ]
    scratch += [dma((NCH,))] * 15
    scratch += [pltpu.SemaphoreType.REGULAR, pltpu.SemaphoreType.REGULAR]
    flops = 6 * R * D * (3 * F + 4 * FQ) * 2
    return pl.pallas_call(
        functools.partial(block_kernel, dims),
        out_shape=(
            jax.ShapeDtypeStruct((T, D), BF),
            jax.ShapeDtypeStruct((T, D), BF),
            jax.ShapeDtypeStruct((4, GROUPS * H, W2), BF),
            late,
            late,
            jax.ShapeDtypeStruct((8, D), F32),
        ),
        in_specs=[hbm] * 7,
        out_specs=(hbm,) * 6,
        scratch_shapes=scratch,
        compiler_params=pltpu.CompilerParams(
            collective_id=0, has_side_effects=True, vmem_limit_bytes=62 * 2**20
        ),
        cost_estimate=pl.CostEstimate(flops=flops, bytes_accessed=60 * 2**20, transcendentals=R * F),
        name="block_kernel",
    )(tokens, cotangent, in_proj, out_proj, gate_up, down_proj, small)


def adamw(weight, first_moment, second_moment, gradient, step_rate, decay_factor):
    first_new = beta_one * first_moment + (1.0 - beta_one) * gradient
    second_new = beta_two * second_moment + (1.0 - beta_two) * gradient * gradient
    adam_ratio = (
        first_new
        / (1.0 - beta_one**STEP)
        / (jnp.sqrt(second_new / (1.0 - beta_two**STEP)) + adam_eps)
    )
    weight_new = weight - step_rate * (adam_ratio + decay_factor * weight)
    return (weight_new, first_new, second_new)


def update_values(rate, w, m, v, grad):
    w, m, v, grad = (a.astype(F32) for a in (w, m, v, grad))
    first = beta_one * m + (1.0 - beta_one) * grad
    second = beta_two * v + (1.0 - beta_two) * grad * grad
    u = second * (1.0 / (1.0 - beta_two**STEP))
    root = u * lax.rsqrt(u) + adam_eps
    return (1.0 - rate * decay_rate) * w - (rate / (1.0 - beta_one**STEP)) * first / root, first, second


def update_gate(rate, where, w, m, v, *refs):
    grads, new = refs[:GROUPS], refs[GROUPS:]
    FG = w.shape[2] // GROUPS
    for g in range(GROUPS):
        cols = slice(FG * g, FG * (g + 1))
        values = update_values(rate, w[0, :, cols], m[0, :, cols], v[0, :, cols], grads[g][0])
        for ref, value in zip(new, values):
            ref[0, :, cols] = value


def update_down(rate, where, w, m, v, *refs):
    one, two, new = refs[:GROUPS], refs[GROUPS : 2 * GROUPS], refs[-3:]
    FG = w.shape[0] // GROUPS
    first = pl.program_id(0) == 0
    for g in range(GROUPS):
        grad = jnp.where(first, one[g][...], two[g][...]).astype(F32)
        for j in range(2):
            at = (slice(FG * g, FG * (g + 1)), slice(CHUNK * j, CHUNK * (j + 1)))
            values = update_values(rate, w[at], m[at], v[at], grad[:, FG * j : FG * (j + 1)].T)
            for ref, value in zip(new, values):
                ref[at] = value


def pick(where, one, two, far_one, far_two):
    c, y = where[0] == 1, where[1] == 1
    near = jnp.where(c, two, one), jnp.where(c, one, two)
    far = jnp.where(c, far_two, far_one), jnp.where(c, far_one, far_two)
    return (
        jnp.where(y, far[0], near[0]), jnp.where(y, far[1], near[1]),
        jnp.where(y, near[0], far[0]), jnp.where(y, near[1], far[1]),
    )


def update_in(rate, where, w, m, v, *refs):
    grads, new = refs[:4], refs[-3:]
    Q = w.shape[1] // 24
    for j in range(6):
        four = pick(where, *(g[:, Q * j : Q * (j + 1)] for g in grads))
        for k in range(4):
            cols = slice((4 * j + k) * Q, (4 * j + k + 1) * Q)
            values = update_values(rate, w[:, cols], m[:, cols], v[:, cols], four[k])
            for ref, value in zip(new, values):
                ref[:, cols] = value


def update_out(rate, where, w, m, v, *refs):
    grads, new = refs[:4], refs[-3:]
    D = w.shape[1]
    Q = w.shape[0] // 4
    FG = grads[0].shape[1] // 2
    for r in range(4):
        for j in range(2):
            cols = slice(D // 2 * j + CHUNK * r, D // 2 * j + CHUNK * (r + 1))
            part = (slice(CHUNK * (r // 2), CHUNK * (r // 2 + 1)), slice(FG * (r % 2) + Q * j, FG * (r % 2) + Q * (j + 1)))
            four = pick(where, *(g[part] for g in grads))
            for k in range(4):
                at = (slice(Q * k, Q * (k + 1)), cols)
                values = update_values(rate, w[at], m[at], v[at], four[k].astype(F32).T)
                for ref, value in zip(new, values):
                    ref[at] = value


def update(kernel, rate, where, state, grads, before, grid, spec, g_specs, name):
    weight = state[0]
    n = grid[0] * grid[1] * spec.block_shape[-1] * spec.block_shape[-2]
    keep = [] if before is None else [pl.BlockSpec(memory_space=pl.ANY)] * 3
    first = 4 + len(grads)
    return pl.pallas_call(
        functools.partial(kernel, rate),
        grid_spec=pltpu.PrefetchScalarGridSpec(
            num_scalar_prefetch=1,
            grid=grid,
            in_specs=[spec] * 3 + list(g_specs) + keep,
            out_specs=(spec,) * 3,
        ),
        out_shape=(jax.ShapeDtypeStruct(weight.shape, F32),) * 3,
        input_output_aliases={} if before is None else {first + i: i for i in range(3)},
        compiler_params=pltpu.CompilerParams(vmem_limit_bytes=56 * 2**20),
        cost_estimate=pl.CostEstimate(flops=12 * n, bytes_accessed=20 * n, transcendentals=2 * n),
        name=name,
    )(where, *state, *grads, *(before or ()))


def fused_body(
    tokens, cotangent, in_proj, in_moment, in_square, out_proj, out_moment, out_square,
    gate_up, gate_moment, gate_square, down_proj, down_moment, down_square,
    conv_kernel, conv_moment, conv_square, norm_gains, gains_moment, gains_square,
):
    T, D = tokens.shape[1:]
    H, Q = D // 2, D // 8
    F = gate_up.shape[2] // 4
    FF, FG = 4 * F, F // GROUPS
    W2 = 2 * FG
    rate = 2.0 * D ** (-0.5)
    down_rate = 2.0 * FF ** (-0.5)
    small = jnp.concatenate(
        [conv_kernel.astype(F32), norm_gains.astype(F32), jnp.zeros((3, H), F32)], axis=0
    )
    block_out, token_grad, grads, mine, other, small_grads = run_block(
        tokens[0], cotangent[0], in_proj, out_proj, gate_up, down_proj, small
    )
    seq = lax.axis_index("seq")
    y, c = seq // 2, seq % 2
    near = jnp.stack([c, y]).astype(jnp.int32)
    far = jnp.stack([c, 1 - y]).astype(jnp.int32)

    gate_state = (gate_up, gate_moment, gate_square)
    down_state = (down_proj, down_moment, down_square)
    in_state = (in_proj, in_moment, in_square)
    out_state = (out_proj, out_moment, out_square)

    def down_step(where, one, two, before, name):
        spec = pl.BlockSpec((F, 2 * CHUNK), lambda k, q, w: (2 * w[1] + w[0] + k * (1 - 2 * w[0]), q))
        g_specs = [pl.BlockSpec((CHUNK, W2), lambda k, q, w, g=g: (2 * g + q * (1 - k) + k, 0)) for g in range(GROUPS)]
        g_specs += [pl.BlockSpec((CHUNK, W2), lambda k, q, w, g=g: (2 * g + q * k, 0)) for g in range(GROUPS)]
        return update(
            update_down, down_rate, where, down_state, (one,) * GROUPS + (two,) * GROUPS, before, (2, 2), spec, g_specs, name
        )

    across = lax.ppermute(mine, "seq", [(i, (i + 2) % 4) for i in range(4)])
    n = H // 256
    gate = update(
        update_gate, rate, near, gate_state, (grads,) * GROUPS, None,
        (2 * n, 4),
        pl.BlockSpec((1, 256, F), lambda r, k, w: (r // n, r % n, k)),
        [pl.BlockSpec((1, 256, FG), lambda r, k, w, g=g: (k, g * n + r % n, r // n)) for g in range(GROUPS)],
        "update_gate",
    )
    down = down_step(near, mine, other, None, "update_down")
    across, gate, down = lax.optimization_barrier((across, gate, down))
    beyond = lax.ppermute(across, "seq", [(i, i + 1 - 2 * (i % 2)) for i in range(4)])
    four = (mine, other, across, beyond)
    down = down_step(far, across, beyond, down, "update_down_far")
    n = 64
    base = GROUPS * H // 2
    inner = update(
        update_in, rate, near, in_state, four, None, (H // n, 1),
        pl.BlockSpec((n, 3 * D), lambda r, k, w: (r, 0)),
        [pl.BlockSpec((n, W2), lambda r, k, w: (base // n + r, 0))] * 4,
        "update_in",
    )
    base += H
    outer = update(
        update_out, rate, near, out_state, four, None, (1, 1),
        pl.BlockSpec((H, D), lambda r, k, w: (0, 0)),
        [pl.BlockSpec((2 * CHUNK, W2), lambda r, k, w: (base // (2 * CHUNK), 0))] * 4,
        "update_out",
    )
    mine_small = lax.dynamic_slice_in_dim(small_grads, lax.axis_index("shard") * H, H, axis=1)
    conv = adamw(
        conv_kernel.astype(F32), conv_moment.astype(F32), conv_square.astype(F32), mine_small[0:3], small_rate, 0.0
    )
    gains = adamw(
        norm_gains.astype(F32), gains_moment.astype(F32), gains_square.astype(F32), mine_small[3:5], small_rate, 0.0
    )
    return (block_out[None], token_grad[None], *inner, *outer, *gate, *down, *conv, *gains)


def shifted(block, axis, distance):
    devices = range(lax.axis_size(axis))
    route = [(i - distance, i) for i in devices if i - distance in devices]
    return lax.ppermute(block, axis, route)


def norm_forward(values, gain_vector):
    norm_scale = lax.rsqrt(jnp.mean(values * values, axis=-1, keepdims=True) + norm_eps)
    unit_rows = values * norm_scale
    return (unit_rows, norm_scale, (unit_rows * gain_vector).astype(jnp.bfloat16))


def norm_backward(grad_normed, unit_rows, norm_scale, gain_vector):
    gain_grad = jnp.sum(grad_normed * unit_rows, axis=(0, 1))
    grad_unit = grad_normed * gain_vector
    grad_values = norm_scale * (
        grad_unit - unit_rows * jnp.mean(grad_unit * unit_rows, axis=-1, keepdims=True)
    )
    return (gain_grad, grad_values)


def plain_body(
    tokens,
    cotangent,
    in_proj,
    in_moment,
    in_square,
    out_proj,
    out_moment,
    out_square,
    gate_up,
    gate_moment,
    gate_square,
    down_proj,
    down_moment,
    down_square,
    conv_kernel,
    conv_moment,
    conv_square,
    norm_gains,
    gains_moment,
    gains_square,
):
    gathered = (
        lax.all_gather(in_proj, "shard", axis=0, tiled=True),
        lax.all_gather(out_proj, "shard", axis=0, tiled=True),
        lax.all_gather(gate_up, "shard", axis=1, tiled=True),
        lax.all_gather(down_proj, "shard", axis=1, tiled=True),
        lax.all_gather(conv_kernel, "shard", axis=1, tiled=True),
        lax.all_gather(norm_gains, "shard", axis=1, tiled=True),
    )
    full_in, full_out, full_gate, full_down, full_conv, full_gains = gathered
    gains_float = full_gains.astype(jnp.float32)
    conv_float = full_conv.astype(jnp.float32)
    inputs = tokens.astype(jnp.float32)
    model_width = inputs.shape[2]
    rows_count = inputs.shape[1]
    unit_one, scale_one, normed_one = norm_forward(inputs, gains_float[0])
    projected = jnp.einsum("scd,de->sce", normed_one, full_in, preferred_element_type=jnp.float32)
    first_gate = projected[:, :, :model_width]
    second_gate = projected[:, :, model_width : 2 * model_width]
    conv_input = projected[:, :, 2 * model_width :]
    mixed_in = (first_gate * conv_input).astype(jnp.bfloat16)
    before = shifted(mixed_in[:, rows_count - 2 :, :], "seq", 1)
    extended = jnp.concatenate([before, mixed_in], axis=1).astype(jnp.float32)
    convolved = (
        conv_float[0] * extended[:, :-2]
        + conv_float[1] * extended[:, 1:-1]
        + conv_float[2] * extended[:, 2:]
    )
    gated_out = (second_gate * convolved).astype(jnp.bfloat16)
    middle = inputs + jnp.einsum(
        "scd,de->sce", gated_out, full_out, preferred_element_type=jnp.float32
    )
    unit_two, scale_two, normed_two = norm_forward(middle, gains_float[1])
    gate_value = jnp.einsum(
        "scd,df->scf", normed_two, full_gate[0], preferred_element_type=jnp.float32
    )
    upward = jnp.einsum("scd,df->scf", normed_two, full_gate[1], preferred_element_type=jnp.float32)
    hidden = (jax.nn.silu(gate_value) * upward).astype(jnp.bfloat16)
    result = middle + jnp.einsum(
        "scf,fd->scd", hidden, full_down, preferred_element_type=jnp.float32
    )
    block_out = result.astype(jnp.bfloat16)
    regathered = (
        lax.all_gather(in_proj, "shard", axis=0, tiled=True),
        lax.all_gather(out_proj, "shard", axis=0, tiled=True),
        lax.all_gather(gate_up, "shard", axis=1, tiled=True),
        lax.all_gather(down_proj, "shard", axis=1, tiled=True),
        lax.all_gather(conv_kernel, "shard", axis=1, tiled=True),
        lax.all_gather(norm_gains, "shard", axis=1, tiled=True),
    )
    full_in, full_out, full_gate, full_down, full_conv, full_gains = regathered
    gains_float = full_gains.astype(jnp.float32)
    conv_float = full_conv.astype(jnp.float32)
    grad_result = cotangent.astype(jnp.float32)
    grad_hidden = jnp.einsum(
        "scd,fd->scf", cotangent, full_down, preferred_element_type=jnp.float32
    )
    grad_down = jnp.einsum("scf,scd->fd", hidden, cotangent, preferred_element_type=jnp.float32)
    sigmoid_gate = jax.nn.sigmoid(gate_value)
    grad_gate = (
        grad_hidden * upward * sigmoid_gate * (1.0 + gate_value * (1.0 - sigmoid_gate))
    ).astype(jnp.bfloat16)
    grad_upward = (grad_hidden * jax.nn.silu(gate_value)).astype(jnp.bfloat16)
    grad_gate_up = jnp.stack(
        [
            jnp.einsum("scd,scf->df", normed_two, grad_gate, preferred_element_type=jnp.float32),
            jnp.einsum("scd,scf->df", normed_two, grad_upward, preferred_element_type=jnp.float32),
        ]
    )
    grad_normed_two = jnp.einsum(
        "scf,df->scd", grad_gate, full_gate[0], preferred_element_type=jnp.float32
    ) + jnp.einsum("scf,df->scd", grad_upward, full_gate[1], preferred_element_type=jnp.float32)
    gain_two, grad_from_two = norm_backward(grad_normed_two, unit_two, scale_two, gains_float[1])
    grad_middle = grad_result + grad_from_two
    middle_low = grad_middle.astype(jnp.bfloat16)
    grad_out = jnp.einsum("scd,sce->de", gated_out, middle_low, preferred_element_type=jnp.float32)
    grad_gated = jnp.einsum("sce,de->scd", middle_low, full_out, preferred_element_type=jnp.float32)
    grad_second = grad_gated * convolved
    grad_conv_out = grad_gated * second_gate
    grad_conv = jnp.stack(
        [
            jnp.sum(grad_conv_out * extended[:, offset : offset + rows_count], axis=(0, 1))
            for offset in range(3)
        ]
    )
    grad_extended = (
        jnp.pad(grad_conv_out * conv_float[0], ((0, 0), (0, 2), (0, 0)))
        + jnp.pad(grad_conv_out * conv_float[1], ((0, 0), (1, 1), (0, 0)))
        + jnp.pad(grad_conv_out * conv_float[2], ((0, 0), (2, 0), (0, 0)))
    )
    from_next = shifted(grad_extended[:, :2, :], "seq", -1)
    grad_mixed = grad_extended[:, 2:, :] + jnp.pad(from_next, ((0, 0), (rows_count - 2, 0), (0, 0)))
    grad_projected = jnp.concatenate(
        [grad_mixed * conv_input, grad_second, grad_mixed * first_gate], axis=2
    ).astype(jnp.bfloat16)
    grad_in = jnp.einsum(
        "scd,sce->de", normed_one, grad_projected, preferred_element_type=jnp.float32
    )
    grad_normed_one = jnp.einsum(
        "sce,de->scd", grad_projected, full_in, preferred_element_type=jnp.float32
    )
    gain_one, grad_from_one = norm_backward(grad_normed_one, unit_one, scale_one, gains_float[0])
    token_grad = (grad_middle + grad_from_one).astype(jnp.bfloat16)
    grad_gains = jnp.stack([gain_one, gain_two])
    parts = (
        lax.psum_scatter(grad_in, "shard", scatter_dimension=0, tiled=True),
        lax.psum_scatter(grad_out, "shard", scatter_dimension=0, tiled=True),
        lax.psum_scatter(grad_gate_up, "shard", scatter_dimension=1, tiled=True),
        lax.psum_scatter(grad_down, "shard", scatter_dimension=1, tiled=True),
        lax.psum_scatter(grad_conv, "shard", scatter_dimension=1, tiled=True),
        lax.psum_scatter(grad_gains, "shard", scatter_dimension=1, tiled=True),
    )
    totals = lax.psum((parts[0], parts[1], parts[2], parts[3], parts[4], parts[5]), ("rep", "seq"))
    matrix_rate = 2.0 * model_width ** (-0.5)
    down_rate = 2.0 * gate_up.shape[2] ** (-0.5)
    in_next, in_moment_next, in_square_next = adamw(
        in_proj.astype(jnp.float32),
        in_moment.astype(jnp.float32),
        in_square.astype(jnp.float32),
        totals[0],
        matrix_rate,
        decay_rate,
    )
    out_next, out_moment_next, out_square_next = adamw(
        out_proj.astype(jnp.float32),
        out_moment.astype(jnp.float32),
        out_square.astype(jnp.float32),
        totals[1],
        matrix_rate,
        decay_rate,
    )
    gate_next, gate_moment_next, gate_square_next = adamw(
        gate_up.astype(jnp.float32),
        gate_moment.astype(jnp.float32),
        gate_square.astype(jnp.float32),
        totals[2],
        matrix_rate,
        decay_rate,
    )
    down_next, down_moment_next, down_square_next = adamw(
        down_proj.astype(jnp.float32),
        down_moment.astype(jnp.float32),
        down_square.astype(jnp.float32),
        totals[3],
        down_rate,
        decay_rate,
    )
    conv_next, conv_moment_next, conv_square_next = adamw(
        conv_kernel.astype(jnp.float32),
        conv_moment.astype(jnp.float32),
        conv_square.astype(jnp.float32),
        totals[4],
        small_rate,
        0.0,
    )
    gains_next, gains_moment_next, gains_square_next = adamw(
        norm_gains.astype(jnp.float32),
        gains_moment.astype(jnp.float32),
        gains_square.astype(jnp.float32),
        totals[5],
        small_rate,
        0.0,
    )
    return (
        block_out,
        token_grad,
        in_next,
        in_moment_next,
        in_square_next,
        out_next,
        out_moment_next,
        out_square_next,
        gate_next,
        gate_moment_next,
        gate_square_next,
        down_next,
        down_moment_next,
        down_square_next,
        conv_next,
        conv_moment_next,
        conv_square_next,
        gains_next,
        gains_moment_next,
        gains_square_next,
    )


def solution(mesh):
    act = P(("rep", "shard"), "seq", None)
    weights = (
        (P("shard", None),) * 6 + (P(None, "shard", None),) * 3 + (P(None, "shard"),) * 9
    )
    specs = (act, act) + weights
    sizes = (mesh.shape["rep"], mesh.shape["seq"], mesh.shape["shard"])
    body = fused_body if sizes == (4, 4, 2) else plain_body
    return jax.shard_map(body, mesh=mesh, in_specs=specs, out_specs=specs, check_vma=False)
```
